256 devices in a mesh: dp: 32 (over z, y_hi, core), expert: 8 (over y_lo, x).
Axes of the slice: x: 4, y: 4 (y_hi: 2, y_lo: 2; y = y_hi * 2 + y_lo), z: 8, core: 2. Of those that a mesh axis runs over, the one named last changes fastest.
Arguments:
- tokens: bfloat16 [1024, 3072], P('expert'), may hold values from -6 to 6
- expert_ids: int32 [1024, 2], P('expert'), may hold values from 0 to 7, all different within a row; in each aligned block of 128 rows (0 to 127, 128 to 255, ...) at most 40 rows name the same one
- combine: float32 [1024, 2], P('expert'), may hold values from 0.1 to 1
- cotangent: bfloat16 [1024, 3072], P('expert'), may hold values from -6 to 6
- w_gate: bfloat16 [8, 3072, 8192], P('expert', None, 'dp'), may hold values from -0.109375 to 0.109375
- w_up: bfloat16 [8, 3072, 8192], P('expert', None, 'dp'), may hold values from -0.109375 to 0.109375
- w_down: bfloat16 [8, 8192, 3072], P('expert', 'dp'), may hold values from -0.0625 to 0.0625
Outputs:
- mixed: bfloat16 [1024, 3072], P('expert', 'dp')
- grad_tokens: bfloat16 [1024, 3072], P('expert', 'dp')
- grad_combine: float32 [1024, 2], P('expert')
- grad_gate: bfloat16 [8, 3072, 8192], P('expert', None, 'dp')
- grad_up: bfloat16 [8, 3072, 8192], P('expert', None, 'dp')
- grad_down: bfloat16 [8, 8192, 3072], P('expert', 'dp')
The draws below stay inside these ranges and needn't reach their ends.
Inputs may be any that keep to these rules, and one draw needn't show every extreme that they name: `expert_ids`: A row names two different experts. Among the rows of one index of expert, each expert is named at most 40 times, a bound that some block reaches.
All inputs are finite; a program needn't handle non-finite values.
Results may differ from the reference program's by a relative error of at most 0.0058.
Values may be sent and summed in bfloat16 or wider, within the bound.
A program may use at most 128 MiB of HBM per device.

```python
import math
import jax
import jax.numpy as jnp
import numpy as np

D = 3072
FF = 8192
TOK_DEV = 128
EXPERTS = 8
CAP = 40
TOKENS = 1024
N_EXPERT = 8


def block_scale(rng, shape, pieces, smallest, high):
    def one(axis_at, shards_of):
        steps = jax.random.uniform(jax.random.fold_in(jax.random.fold_in(rng, 6), axis_at), (shards_of,), jnp.float32, smallest / len(pieces), high / len(pieces))
        return jnp.repeat(jnp.exp(steps), shape[axis_at] // shards_of).reshape((-1,) + (1,) * (len(shape) - axis_at - 1))

    level = one(*pieces[0])
    for cut in pieces[1:]:
        level = level * one(*cut)
    return level


def deal_out(rng, own, number, rows, count, top, most, lean):
    ranking = jax.random.permutation(rng, count)
    crowded, usual = load_shares(count, rows * top, most, lean, True), load_shares(count, rows * top, most, lean, False)
    places = jnp.arange(count)

    def named(tallies, offset_by):
        used = int((tallies > 0).sum())
        fixed = max(1, used // 4)
        passed = fixed + (places - fixed + offset_by * (used - fixed)) % max(1, count - fixed)
        return jnp.zeros((count,), jnp.int32).at[ranking[jnp.where(places < fixed, places, passed)]].set(jnp.asarray(tallies, jnp.int32))

    tallies = jnp.where(number % 4 == 0, named(crowded, number // 4), named(usual, number - number // 4 - 1))
    mixed = jax.random.permutation(jax.random.fold_in(own, 3), count)
    donor, taker = mixed[0:count // 2 * 2:2], mixed[1:count // 2 * 2:2]
    room = jnp.minimum(tallies[donor] - 1, most - tallies[taker]) // 2
    room = jnp.where((donor == ranking[0]) | (taker == ranking[0]) | (tallies[taker] == 0), 0, jnp.maximum(room, 0))
    passed = jax.random.randint(jax.random.fold_in(own, 4), (count // 2,), 0, 1 << 20) % (room + 1)
    tallies = tallies.at[donor].add(-passed).at[taker].add(passed)
    labels = jnp.searchsorted(jnp.cumsum(tallies), jnp.arange(rows * top), side="right").astype(jnp.int32)
    listing = labels.reshape(top, rows).T
    listing = listing[jax.random.permutation(jax.random.fold_in(own, 1), rows)]
    offset_by = jax.random.randint(jax.random.fold_in(own, 2), (rows, 1), 0, top)
    return jnp.take_along_axis(listing, (jnp.arange(top)[None, :] + offset_by) % top, axis=1)


def load_shares(count, total, reach, skew, full):
    weights = [(1 << 20) // math.isqrt(rank ** skew) + 1 for rank in range(1, count + 1)]
    largest = reach if full else min(reach, max(-(-total // count), total * weights[0] // sum(weights)))
    least = 1 if total - largest >= count - 1 else 0
    given, rest = [largest] + [least] * (count - 1), total - largest - least * (count - 1)
    while rest > 0:
        free = [i for i in range(1, count) if given[i] < largest] or [i for i in range(1, count) if given[i] < reach]
        pool, remaining = sum([weights[i] for i in free]), rest
        for i in free:
            addition = min(reach - given[i], max(1, remaining * weights[i] // pool), rest)
            given[i] = given[i] + addition
            rest = rest - addition
    return np.array(given)


def noise(own_key, shape, scale, most, cuts=(), kind=jnp.bfloat16):
    values = scale * jax.random.normal(own_key, shape, jnp.float32)
    if cuts:
        values = values * block_scale(own_key, shape, cuts, -0.22, 0.18)
    return jnp.clip(values, -most, most).astype(kind)


def setup_inputs(seed: int = 0) -> dict:
    splits = jax.random.split(jax.random.key(seed), 8)
    tokens = noise(splits[0], (TOKENS, D), 1.0, 6.0, ((0, 8),))
    expert_ids_keys = jax.random.split(jax.random.fold_in(splits[1], 1), TOKENS // TOK_DEV)
    expert_ids_turns = jax.random.permutation(jax.random.fold_in(splits[1], 3), TOKENS // TOK_DEV)
    expert_ids = jax.vmap(lambda own, number: deal_out(jax.random.fold_in(splits[1], 2), own, number, TOK_DEV, EXPERTS, 2, CAP, 1))(expert_ids_keys, expert_ids_turns).reshape((TOKENS, 2))
    combine = jnp.clip(0.1 + 0.9 * jax.random.uniform(splits[2], (TOKENS, 2), jnp.float32) ** block_scale(splits[2], (TOKENS, 2), ((0, 8),), -0.2, 0.2), 0.1, 1.0)
    cotangent = noise(splits[3], (TOKENS, D), 1.0, 6.0, ((0, 8),))
    w_gate = noise(splits[4], (EXPERTS, D, FF), D ** -0.5, 0.109375, ((0, 8), (2, 32)))
    w_up = noise(splits[5], (EXPERTS, D, FF), D ** -0.5, 0.109375, ((0, 8), (2, 32)))
    w_down = noise(splits[6], (EXPERTS, FF, D), FF ** -0.5, 0.0625, ((0, 8), (1, 32)))
    return dict(tokens=tokens, expert_ids=expert_ids, combine=combine, cotangent=cotangent, w_gate=w_gate, w_up=w_up, w_down=w_down)


def expert_pass(x_rows, e_rows, gate_w, up_w, down_w):
    gate_proj = jnp.dot(x_rows, gate_w, preferred_element_type=jnp.float32)
    up_proj = jnp.dot(x_rows, up_w, preferred_element_type=jnp.float32)
    sigmoid_g = jax.nn.sigmoid(gate_proj)
    active = gate_proj * sigmoid_g
    hidden = (active * up_proj).astype(jnp.bfloat16)
    out_rows = jnp.dot(hidden, down_w, preferred_element_type=jnp.float32)
    hidden_grad = jnp.dot(e_rows, down_w.T, preferred_element_type=jnp.float32)
    gate_grad = (hidden_grad * up_proj * sigmoid_g * (1.0 + gate_proj * (1.0 - sigmoid_g))).astype(jnp.bfloat16)
    up_grad = (hidden_grad * active).astype(jnp.bfloat16)
    down_sum = jnp.dot(hidden.T, e_rows, preferred_element_type=jnp.float32)
    gate_sum = jnp.dot(x_rows.T, gate_grad, preferred_element_type=jnp.float32)
    up_sum = jnp.dot(x_rows.T, up_grad, preferred_element_type=jnp.float32)
    input_grad = jnp.dot(gate_grad, gate_w.T, preferred_element_type=jnp.float32) + jnp.dot(up_grad, up_w.T, preferred_element_type=jnp.float32)
    return out_rows, input_grad, gate_sum, up_sum, down_sum


def reference(tokens, expert_ids, combine, cotangent, w_gate, w_up, w_down):
    token_count = tokens.shape[0]
    limit = N_EXPERT * CAP
    mixed_sum = jnp.zeros((token_count, D), jnp.float32)
    input_sum = jnp.zeros((token_count, D), jnp.float32)
    combine_grad = jnp.zeros((token_count, 2), jnp.float32)
    cot_float = cotangent.astype(jnp.float32)
    gate_list, up_list, down_list = [], [], []
    for expert in range(EXPERTS):
        chosen = expert_ids == expert
        picked_mask = jnp.any(chosen, axis=1)
        weight = jnp.sum(jnp.where(chosen, combine, jnp.zeros_like(combine)), axis=1)
        row_index = jnp.nonzero(picked_mask, size=limit, fill_value=0)[0].astype(jnp.int32)
        live_count = jnp.sum(picked_mask.astype(jnp.int32))
        is_live = (jnp.arange(limit, dtype=jnp.int32) < live_count)[:, None]
        x_rows = jnp.where(is_live, tokens[row_index], jnp.zeros((), tokens.dtype)).astype(jnp.bfloat16)
        e_float = cot_float[row_index] * weight[row_index][:, None]
        e_rows = jnp.where(is_live, e_float, jnp.zeros_like(e_float)).astype(jnp.bfloat16)
        out_rows, input_grad, gate_sum, up_sum, down_sum = expert_pass(x_rows, e_rows, w_gate[expert], w_up[expert], w_down[expert])
        zero_tok = jnp.zeros((token_count, D), jnp.float32)
        out_tok = zero_tok.at[row_index].add(jnp.where(is_live, out_rows, jnp.zeros_like(out_rows)))
        in_tok = zero_tok.at[row_index].add(jnp.where(is_live, input_grad, jnp.zeros_like(input_grad)))
        mixed_sum = mixed_sum + weight[:, None] * out_tok
        input_sum = input_sum + in_tok
        dot_tok = jnp.sum(cot_float * out_tok, axis=1)
        combine_grad = combine_grad + jnp.where(chosen, dot_tok[:, None], jnp.zeros_like(combine_grad))
        gate_list.append(gate_sum.astype(jnp.bfloat16))
        up_list.append(up_sum.astype(jnp.bfloat16))
        down_list.append(down_sum.astype(jnp.bfloat16))
    return (mixed_sum.astype(jnp.bfloat16), input_sum.astype(jnp.bfloat16), combine_grad,
            jnp.stack(gate_list), jnp.stack(up_list), jnp.stack(down_list))
```

```python
import jax
import jax.numpy as jnp
from jax import lax
from jax.experimental import pallas as pl
from jax.experimental.pallas import tpu as pltpu
from jax.sharding import PartitionSpec as P

MESH = pl.DeviceIdType.MESH
F32 = jnp.float32
BF16 = jnp.bfloat16

T = 128
D = 3072
HD = 1536
CAP = 40
BLK = 2 * CAP
SLAB = 48
NE = 8
NZ = 8
W = 256
CH = 384
NP = 4

PLANE = ((2, 1), (1, 1), (3, 1), (2, 0), (0, 1), (1, 0), (3, 0))


def nn(a, b):
    return lax.dot_general(a, b, (((1,), (0,)), ((), ())), preferred_element_type=F32)


def nt(a, b):
    return lax.dot_general(a, b, (((1,), (1,)), ((), ())), preferred_element_type=F32)


def tn(a, b):
    return lax.dot_general(a, b, (((0,), (0,)), ((), ())), preferred_element_type=F32)


def iota(shape, axis):
    return lax.broadcasted_iota(jnp.int32, shape, axis)


def split3(a):
    hi = a.astype(BF16)
    rest = a - hi.astype(F32)
    mid = rest.astype(BF16)
    low = (rest - mid.astype(F32)).astype(BF16)
    return hi, mid, low


def kernel(
    tok_hbm, ids_ref, comb_ref, cot_hbm, wg_hbm, wu_hbm, wd_hbm,
    mixed_ref, gtok_ref, gcomb_ref, gg_hbm, gu_hbm, gd_hbm,
    tc, wg, wu, wd, wgx, wux, wdx, slt, cwt, sendb, rows, acts, actx,
    gsend, grecv, tmat, rsend, rrecv, zsend, zrecv, gzrecv, ysend, yrecv, gycs,
    fsend, frecv, og, ou, od,
    lsem, osem, ws_s, ws_r, d_s, d_r, c_s, c_r, x_s, x_r, g_s, g_r, r_s, r_r,
    z_s, z_r, gz_s, gz_r, p_s, p_r,
):
    d = lax.axis_index("dp")
    e = lax.axis_index("expert")
    z, h, c = d // 4, (d // 2) % 2, d % 2
    yl, x = e // 4, e % 4
    twin = (z * 4 + h * 2 + (1 - c), e)
    over = (z * 4 + (1 - h) * 2 + c, e)

    def plane(step):
        return ((yl + step[1]) % 2) * 4 + (x + step[0]) % 4

    def at_z(k):
        return (z + k) % NZ

    def zdev(zz):
        return (zz * 4 + h * 2 + c, e)

    def remote(src, dst, ssem, rsem, dev):
        return pltpu.make_async_remote_copy(
            src_ref=src, dst_ref=dst, send_sem=ssem, recv_sem=rsem, device_id=dev, device_id_type=MESH
        )

    half = pl.multiple_of(c * HD, HD)
    other_half = pl.multiple_of((1 - c) * HD, HD)

    loads = [
        pltpu.make_async_copy(tok_hbm.at[:, pl.ds(half, HD)], tc.at[pl.ds(0, T)], lsem.at[0]),
        pltpu.make_async_copy(cot_hbm.at[:, pl.ds(half, HD)], tc.at[pl.ds(T, T)], lsem.at[1]),
        pltpu.make_async_copy(wg_hbm, wg, lsem.at[2]),
        pltpu.make_async_copy(wu_hbm, wu, lsem.at[3]),
        pltpu.make_async_copy(wd_hbm, wd, lsem.at[4]),
    ]
    for cp in loads:
        cp.start()

    barrier = pltpu.get_barrier_semaphore()
    for step in PLANE:
        pl.semaphore_signal(barrier, inc=1, device_id=(d, plane(step)), device_id_type=MESH)
    for k in range(1, NZ):
        pl.semaphore_signal(barrier, inc=1, device_id=zdev(at_z(k)), device_id_type=MESH)
    pl.semaphore_signal(barrier, inc=1, device_id=twin, device_id_type=MESH)
    pl.semaphore_signal(barrier, inc=1, device_id=over, device_id_type=MESH)

    lane = iota((T, T), 1)
    ids = ids_ref[...]
    comb = comb_ref[...]
    pick0 = lane == ids[:, 0:1]
    pick1 = lane == ids[:, 1:2]
    chosen = jnp.logical_or(pick0, pick1)
    earlier = (iota((T, T), 0) > lane).astype(F32).astype(BF16)
    rank = nn(earlier, chosen.astype(F32).astype(BF16))
    slot = jnp.where(chosen, rank, -128.0)
    weight = jnp.where(pick0, comb[:, 0:1], 0.0) + jnp.where(pick1, comb[:, 1:2], 0.0)
    slot_t = slot.T
    weight_t = weight.T
    slt[...] = jnp.concatenate([slot_t[0:NE], slot_t[0:NE]], axis=1)
    cwt[...] = jnp.concatenate([jnp.ones((NE, T), F32), weight_t[0:NE]], axis=1)

    loads[0].wait()
    loads[1].wait()
    pl.semaphore_wait(barrier, len(PLANE) + NZ - 1 + 2)

    def pack(j):
        slots = slt[pl.ds(j, 1), :]
        weights = cwt[pl.ds(j, 1), :]
        row = iota((BLK, 2 * T), 0)
        col = iota((BLK, 2 * T), 1)
        want = jnp.where(col < T, row, row - CAP).astype(F32)
        hit = want == slots
        scale = jnp.sum(jnp.where(hit, weights, 0.0), axis=1, keepdims=True)
        block = nn(hit.astype(F32).astype(BF16), tc[...])
        sendb[j] = (block * scale).astype(BF16)

    sends = []
    for i, step in enumerate(PLANE):
        j = plane(step)
        pack(j)
        cp = remote(sendb.at[j], rows.at[c, e], d_s.at[i], d_r.at[e], (d, j))
        cp.start()
        sends.append(cp)
    pack(e)
    own = pltpu.make_async_copy(sendb.at[e], rows.at[c, e], lsem.at[5])
    own.start()
    cp = remote(sendb.at[e], rows.at[c, e], c_s.at[7], c_r.at[e], twin)
    cp.start()
    sends.append(cp)

    for m in range(NP):
        for n, (src, dst) in enumerate((
            (wd_hbm.at[:, pl.ds(pl.multiple_of((2 * m + 1 - c) * CH, CH), CH)], wdx.at[m]),
            (wg_hbm.at[pl.ds(pl.multiple_of((2 * m + c) * CH, CH), CH)], wgx.at[m]),
            (wu_hbm.at[pl.ds(pl.multiple_of((2 * m + c) * CH, CH), CH)], wux.at[m]),
        )):
            cp = remote(src, dst, ws_s.at[n, m], ws_r.at[n, m], twin)
            cp.start()
            sends.append(cp)

    expand = (iota((T, NE * BLK), 0) == iota((T, NE * BLK), 1) // BLK).astype(F32).astype(BF16)
    w_hi = weight.astype(BF16)
    w_lo = (weight - w_hi.astype(F32)).astype(BF16)
    inner = (iota((T, NE * BLK), 1) % BLK).astype(F32)
    slots_all = nn(slot.astype(BF16), expand)
    out_hit = slots_all == inner
    tmat[0:T] = jnp.where(out_hit, nn(w_hi, expand), 0.0).astype(BF16)
    tmat[T:2 * T] = jnp.where(out_hit, nn(w_lo, expand), 0.0).astype(BF16)
    tmat[2 * T:3 * T] = (slots_all == inner - CAP).astype(F32).astype(BF16)

    for i, step in enumerate(PLANE):
        j = plane((4 - step[0], step[1]))
        here = rows.at[c, j]
        remote(here, here, d_s.at[i], d_r.at[j], (d, j)).wait_recv()
        cp = remote(here, here, c_s.at[i], c_r.at[j], twin)
        cp.start()
        sends.append(cp)
    own.wait()
    for cp in loads[2:]:
        cp.wait()
    for i, step in enumerate(PLANE + ((0, 0),)):
        j = plane((4 - step[0], step[1]))
        there = rows.at[1 - c, j]
        remote(there, there, c_s.at[i], c_r.at[j], twin).wait_recv()

    def x_rows(k):
        return rows[k, :, 0:SLAB, :].reshape(NE * SLAB, HD)

    def e_rows(k):
        return rows[k, :, BLK - SLAB:BLK, :].reshape(NE * SLAB, HD)

    def first(a):
        return a.reshape(NE, SLAB, W)[:, 0:CAP].reshape(NE * CAP, W)

    def last(a):
        return a.reshape(NE, SLAB, W)[:, SLAB - CAP:].reshape(NE * CAP, W)

    gate = first(nn(x_rows(0), wg[0:HD]) + nn(x_rows(1), wg[HD:D]))
    up = first(nn(x_rows(0), wu[0:HD]) + nn(x_rows(1), wu[HD:D]))
    hgrad = last(nt(e_rows(0), wd[:, 0:HD]) + nt(e_rows(1), wd[:, HD:D]))
    sig = jax.nn.sigmoid(gate)
    active = gate * sig
    hidden = (active * up).astype(BF16)
    gate_grad = (hgrad * up * sig * (1.0 + gate * (1.0 - sig))).astype(BF16)
    up_grad = (hgrad * active).astype(BF16)
    acts[0] = hidden
    acts[1] = gate_grad
    acts[2] = up_grad
    xact = remote(acts, actx, x_s, x_r, twin)
    xact.start()
    hid32 = hidden.astype(F32)
    dots = jnp.sum(hid32 * hgrad, axis=1, keepdims=True)
    gsend[...] = jnp.broadcast_to(dots, (NE * CAP, T)).reshape(NE, CAP, T)
    for i, step in enumerate(PLANE):
        j = plane(step)
        cp = remote(gsend.at[j], grecv.at[e], g_s.at[i], g_r.at[e], (d, j))
        cp.start()
        sends.append(cp)
    grecv[e] = gsend[e]
    for n in range(3):
        for m in range(NP):
            cp = remote(
                (wdx, wgx, wux)[n].at[m], (wdx, wgx, wux)[n].at[m], ws_s.at[n, m], ws_r.at[n, m], twin
            )
            cp.wait_recv()
    xact.wait_recv()

    for s in range(NP):
        m = (z // 2 + s + 1) % NP
        oc = pl.multiple_of((2 * m + c) * CH, CH)
        tcol = pl.multiple_of((2 * m + 1 - c) * CH, CH)
        out = nn(acts[0], wd[:, pl.ds(oc, CH)]) + nn(actx[0], wdx[m])
        back = (
            nt(acts[1], wg[pl.ds(tcol, CH), :]) + nt(acts[2], wu[pl.ds(tcol, CH), :])
            + nt(actx[1], wgx[m]) + nt(actx[2], wux[m])
        )
        both = jnp.concatenate([out.reshape(NE, CAP, CH), back.reshape(NE, CAP, CH)], axis=1)
        rsend[s] = both.astype(BF16)
        for i, step in enumerate(PLANE):
            j = plane(step)
            cp = remote(rsend.at[s, j], rrecv.at[s, e], r_s.at[s, i], r_r.at[s, e], (d, j))
            cp.start()
            sends.append(cp)
        rrecv[s, e] = rsend[s, e]

    for step in PLANE:
        j = plane((4 - step[0], step[1]))
        remote(gsend.at[j], grecv.at[j], g_s.at[0], g_r.at[j], (d, j)).wait_recv()
    q = iota((T, NE * CAP), 1).astype(F32)
    place0 = jnp.sum(jnp.where(pick0, lane.astype(F32) * CAP + rank, 0.0), axis=1, keepdims=True)
    place1 = jnp.sum(jnp.where(pick1, lane.astype(F32) * CAP + rank, 0.0), axis=1, keepdims=True)
    hits = jnp.concatenate([(q == place0), (q == place1)], axis=0).astype(F32).astype(BF16)
    parts = split3(grecv[...].reshape(NE * CAP, T))
    got = nn(hits, parts[0]) + nn(hits, parts[1]) + nn(hits, parts[2])
    col0 = got[0:T] / comb[:, 0:1]
    col1 = got[T:2 * T] / comb[:, 1:2]
    two = jnp.where(lane == 0, col0, jnp.where(lane == 1, col1, 0.0))
    gzrecv[z] = two.T[0:8]
    for k in range(1, NZ):
        cp = remote(gzrecv.at[z], gzrecv.at[z], gz_s.at[k], gz_r.at[z], zdev(at_z(k)))
        cp.start()
        sends.append(cp)

    def padded(a, lead):
        a = a.astype(F32).reshape(NE, CAP, W)
        zero = jnp.zeros((NE, SLAB - CAP, W), F32)
        a = jnp.concatenate([a, zero] if lead else [zero, a], axis=1)
        return a.reshape(NE * SLAB, W).astype(BF16)

    hid_pad = padded(acts[0], False)
    pair_pad = jnp.concatenate([padded(acts[1], True), padded(acts[2], True)], axis=1)
    stores = []
    for k in range(2):
        both = tn(x_rows(k), pair_pad)
        og[k * HD:(k + 1) * HD] = both[:, 0:W].astype(BF16)
        ou[k * HD:(k + 1) * HD] = both[:, W:2 * W].astype(BF16)
        od[:, k * HD:(k + 1) * HD] = tn(hid_pad, e_rows(k)).astype(BF16)
    for n, (src, dst) in enumerate(((og, gg_hbm), (ou, gu_hbm), (od, gd_hbm))):
        cp = pltpu.make_async_copy(src, dst, osem.at[n])
        cp.start()
        stores.append(cp)

    mine = z % 2 == c
    for s in range(NP):
        for step in PLANE:
            j = plane((4 - step[0], step[1]))
            remote(rsend.at[s, j], rrecv.at[s, j], r_s.at[s, 0], r_r.at[s, j], (d, j)).wait_recv()
        m = (z // 2 + s + 1) % NP
        sums = nn(tmat[...], rrecv[s].reshape(NE * BLK, CH))
        mix = sums[0:T] + sums[T:2 * T]
        back = sums[2 * T:3 * T]
        if s < NP - 1:
            zsend[s, 0] = mix.astype(BF16)
            zsend[s, 1] = back.astype(BF16)
            for n in range(2):
                to = 2 * m + (c if n == 0 else 1 - c)
                cp = remote(zsend.at[s, n], zrecv.at[z], z_s.at[s, n], z_r.at[z], zdev(to))
                cp.start()
                sends.append(cp)
        else:
            zsend[s, 0] = jnp.where(mine, back, mix).astype(BF16)
            to = z + 1 - 2 * (z % 2)
            cp = remote(zsend.at[s, 0], zrecv.at[z], z_s.at[s, 0], z_r.at[z], zdev(to))
            cp.start()
            sends.append(cp)
            total = jnp.where(mine, mix, back)

    for k in range(1, NZ):
        zz = at_z(k)
        remote(gzrecv.at[zz], gzrecv.at[zz], gz_s.at[k], gz_r.at[zz], zdev(zz)).wait_recv()
    gc_sum = gzrecv[0]
    for k in range(1, NZ):
        gc_sum = gc_sum + gzrecv[k]
    gycs[0] = gc_sum
    gy = remote(gycs.at[0], gycs.at[1], p_s.at[0], p_r.at[0], over)
    gy.start()
    for k in range(1, NZ):
        zz = at_z(k)
        remote(zsend.at[0, 0], zrecv.at[zz], z_s.at[0, 0], z_r.at[zz], zdev(zz)).wait_recv()
        total = total + zrecv[zz].astype(F32)
    ysend[...] = total.astype(BF16)
    theirs = pl.ds(pl.multiple_of(T * (1 - h), T), 2 * T)
    yc = remote(ysend.at[:, theirs], yrecv, p_s.at[1], p_r.at[1], over)
    yc.start()
    gy.wait_recv()
    gc_sum = gc_sum + gycs[1]
    gycs[2] = gc_sum
    gx = remote(gycs.at[2], gycs.at[3], p_s.at[2], p_r.at[2], twin)
    gx.start()
    yc.wait_recv()
    window = jnp.where(h == 0, total[:, 0:2 * T], total[:, T:3 * T])
    final = (window + yrecv[...].astype(F32)).astype(BF16)
    fsend[...] = final
    fc = remote(fsend, frecv, p_s.at[3], p_r.at[3], twin)
    fc.start()
    shift = 64 * h + 96 * c
    pick = (iota((2 * T, T), 0) == iota((2 * T, T), 1) + shift).astype(F32).astype(BF16)
    gx.wait_recv()
    gc_sum = gc_sum + gycs[3]
    square = jnp.concatenate([gc_sum, jnp.zeros((T - 8, T), F32)], axis=0)
    gcomb_ref[...] = square.T[:, 0:2]
    a = nn(final, pick)
    fc.wait_recv()
    b = nn(frecv[...], pick)
    mixed_ref[...] = jnp.where(mine, a, b)[:, 0:96].astype(BF16)
    gtok_ref[...] = jnp.where(mine, b, a)[:, 0:96].astype(BF16)

    for cp in sends:
        cp.wait_send()
    for cp in (xact, gy, yc, gx, fc):
        cp.wait_send()
    for cp in stores:
        cp.wait()


def local(tokens, expert_ids, combine, cotangent, w_gate, w_up, w_down):
    any_spec = pl.BlockSpec(memory_space=pl.ANY)
    vmem = pl.BlockSpec(memory_space=pltpu.VMEM)
    dma = pltpu.SemaphoreType.DMA
    mixed, gtok, gcomb, gg, gu, gd = pl.pallas_call(
        kernel,
        out_shape=(
            jax.ShapeDtypeStruct((T, 96), BF16),
            jax.ShapeDtypeStruct((T, 96), BF16),
            jax.ShapeDtypeStruct((T, 2), F32),
            jax.ShapeDtypeStruct((D, W), BF16),
            jax.ShapeDtypeStruct((D, W), BF16),
            jax.ShapeDtypeStruct((W, D), BF16),
        ),
        in_specs=[any_spec, vmem, vmem, any_spec, any_spec, any_spec, any_spec],
        out_specs=(vmem, vmem, vmem, any_spec, any_spec, any_spec),
        scratch_shapes=[
            pltpu.VMEM((2 * T, HD), BF16),
            pltpu.VMEM((D, W), BF16),
            pltpu.VMEM((D, W), BF16),
            pltpu.VMEM((W, D), BF16),
            pltpu.VMEM((NP, CH, W), BF16),
            pltpu.VMEM((NP, CH, W), BF16),
            pltpu.VMEM((NP, W, CH), BF16),
            pltpu.VMEM((NE, 2 * T), F32),
            pltpu.VMEM((NE, 2 * T), F32),
            pltpu.VMEM((NE, BLK, HD), BF16),
            pltpu.VMEM((2, NE, BLK, HD), BF16),
            pltpu.VMEM((3, NE * CAP, W), BF16),
            pltpu.VMEM((3, NE * CAP, W), BF16),
            pltpu.VMEM((NE, CAP, T), F32),
            pltpu.VMEM((NE, CAP, T), F32),
            pltpu.VMEM((3 * T, NE * BLK), BF16),
            pltpu.VMEM((NP, NE, BLK, CH), BF16),
            pltpu.VMEM((NP, NE, BLK, CH), BF16),
            pltpu.VMEM((NP, 2, T, CH), BF16),
            pltpu.VMEM((NZ, T, CH), BF16),
            pltpu.VMEM((NZ, 8, T), F32),
            pltpu.VMEM((T, CH), BF16),
            pltpu.VMEM((T, 2 * T), BF16),
            pltpu.VMEM((4, 8, T), F32),
            pltpu.VMEM((T, 2 * T), BF16),
            pltpu.VMEM((T, 2 * T), BF16),
            pltpu.VMEM((D, W), BF16),
            pltpu.VMEM((D, W), BF16),
            pltpu.VMEM((W, D), BF16),
            dma((6,)),
            dma((3,)),
            dma((3, NP)),
            dma((3, NP)),
            dma((7,)),
            dma((NE,)),
            dma((8,)),
            dma((NE,)),
            dma,
            dma,
            dma((7,)),
            dma((NE,)),
            dma((NP, 7)),
            dma((NP, NE)),
            dma((NP, 2)),
            dma((NZ,)),
            dma((NZ,)),
            dma((NZ,)),
            dma((4,)),
            dma((4,)),
        ],
        compiler_params=pltpu.CompilerParams(
            collective_id=0, has_side_effects=True, vmem_limit_bytes=60 * 1024 * 1024
        ),
        name="moe_layer",
    )(tokens, expert_ids, combine, cotangent, w_gate[0], w_up[0], w_down[0])
    return mixed, gtok, gcomb, gg[None], gu[None], gd[None]


def solution(mesh):
    in_specs = (
        P("expert", None),
        P("expert", None),
        P("expert", None),
        P("expert", None),
        P("expert", None, "dp"),
        P("expert", None, "dp"),
        P("expert", "dp", None),
    )
    out_specs = (
        P("expert", "dp"),
        P("expert", "dp"),
        P("expert", None),
        P("expert", None, "dp"),
        P("expert", None, "dp"),
        P("expert", "dp", None),
    )
    return jax.shard_map(local, mesh=mesh, in_specs=in_specs, out_specs=out_specs, check_vma=False)
```

```python
import jax
import jax.numpy as jnp
from jax import lax
from jax.experimental import pallas as pl
from jax.experimental.pallas import tpu as pltpu
from jax.sharding import PartitionSpec as P

MESH = pl.DeviceIdType.MESH
F32 = jnp.float32
BF16 = jnp.bfloat16

T = 128
D = 3072
HD = 1536
QD = 768
CAP = 40
BLK = 2 * CAP
SLAB = 48
NE = 8
NZ = 8
W = 256
CH = 384
NP = 4

FAR = (2, 1, 3, 0)

PLANE = ((2, 1), (1, 1), (3, 1), (2, 0), (0, 1), (1, 0), (3, 0))


def nn(a, b):
    return lax.dot_general(a, b, (((1,), (0,)), ((), ())), preferred_element_type=F32)


def nt(a, b):
    return lax.dot_general(a, b, (((1,), (1,)), ((), ())), preferred_element_type=F32)


def tn(a, b):
    return lax.dot_general(a, b, (((0,), (0,)), ((), ())), preferred_element_type=F32)


def iota(shape, axis):
    return lax.broadcasted_iota(jnp.int32, shape, axis)


def kernel(
    tok_hbm, ids_ref, comb_ref, cot_hbm, wg_hbm, wu_hbm, wd_hbm,
    mixed_ref, gtok_ref, gcomb_ref, gg_hbm, gu_hbm, gd_hbm,
    tc, wg, wu, wd, wgx, wux, wdx, slt, cwt, sendb, rows, acts, actx,
    gsend, grecv, tmat, rsend, rrecv, zsend, zrecv, gzrecv, ysend, yrecv, gycs,
    fsend, frecv, og, ou, od,
    lsem, osem, ws_s, ws_r, d_s, d_r, n_s, n_r, c_s, c_r, x_s, x_r, g_s, g_r, r_s, r_r,
    z_s, z_r, gz_s, gz_r, y_s, y_r, p_s, p_r,
):
    d = lax.axis_index("dp")
    e = lax.axis_index("expert")
    z, h, c = d // 4, (d // 2) % 2, d % 2
    yl, x = e // 4, e % 4
    twin = (z * 4 + h * 2 + (1 - c), e)
    over = (z * 4 + (1 - h) * 2 + c, e)

    def plane(step):
        return ((yl + step[1]) % 2) * 4 + (x + step[0]) % 4

    def at_z(k):
        return (z + k) % NZ

    def zdev(zz):
        return (zz * 4 + h * 2 + c, e)

    def remote(src, dst, ssem, rsem, dev):
        return pltpu.make_async_remote_copy(
            src_ref=src, dst_ref=dst, send_sem=ssem, recv_sem=rsem, device_id=dev, device_id_type=MESH
        )

    par = z % 2
    quarter = pl.multiple_of(c * HD + par * QD, QD)
    mate = z + 1 - 2 * par
    mate_over = (mate * 4 + (1 - h) * 2 + c, e)
    near = (zdev(mate), zdev((z + 2 * par + NZ - 1) % NZ))

    loads = [
        pltpu.make_async_copy(tok_hbm.at[:, pl.ds(quarter, QD)], tc.at[pl.ds(0, T)], lsem.at[0]),
        pltpu.make_async_copy(cot_hbm.at[:, pl.ds(quarter, QD)], tc.at[pl.ds(T, T)], lsem.at[1]),
        pltpu.make_async_copy(wg_hbm, wg, lsem.at[2]),
        pltpu.make_async_copy(wu_hbm, wu, lsem.at[3]),
        pltpu.make_async_copy(wd_hbm, wd, lsem.at[4]),
    ]
    for cp in loads:
        cp.start()

    barrier = pltpu.get_barrier_semaphore()
    for step in PLANE:
        pl.semaphore_signal(barrier, inc=1, device_id=(d, plane(step)), device_id_type=MESH)
    for k in range(1, NZ):
        pl.semaphore_signal(barrier, inc=1, device_id=zdev(at_z(k)), device_id_type=MESH)
    pl.semaphore_signal(barrier, inc=1, device_id=twin, device_id_type=MESH)
    pl.semaphore_signal(barrier, inc=1, device_id=over, device_id_type=MESH)
    pl.semaphore_signal(barrier, inc=1, device_id=mate_over, device_id_type=MESH)

    deep = iota((T, T), 0)
    lane = iota((T, T), 1)
    ids = ids_ref[...]
    comb = comb_ref[...]
    pick0 = deep == ids[0:1]
    pick1 = deep == ids[1:2]
    chosen = jnp.logical_or(pick0, pick1)
    earlier = (deep < lane).astype(F32).astype(BF16)
    rank = nn(chosen.astype(F32).astype(BF16), earlier)
    slot = jnp.where(chosen, rank, -128.0)
    weight = jnp.where(pick0, comb[0:1], 0.0) + jnp.where(pick1, comb[1:2], 0.0)
    slt[...] = jnp.concatenate([slot[0:NE], slot[0:NE]], axis=1)
    cwt[...] = jnp.concatenate([jnp.ones((NE, T), F32), weight[0:NE]], axis=1)

    loads[0].wait()
    loads[1].wait()
    pl.semaphore_wait(barrier, len(PLANE) + NZ - 1 + 3)

    def pack(j):
        slots = slt[pl.ds(j, 1), :]
        weights = cwt[pl.ds(j, 1), :]
        row = iota((BLK, 2 * T), 0)
        col = iota((BLK, 2 * T), 1)
        want = jnp.where(col < T, row, row - CAP).astype(F32)
        hit = want == slots
        scale = jnp.sum(jnp.where(hit, weights, 0.0), axis=1, keepdims=True)
        block = nn(hit.astype(F32).astype(BF16), tc[...])
        sendb[j] = (block * scale).astype(BF16)

    sends = []
    for i, step in enumerate(PLANE):
        j = plane(step)
        pack(j)
        cp = remote(sendb.at[j], rows.at[c, par, e], d_s.at[i], d_r.at[e], (d, j))
        cp.start()
        sends.append(cp)
    pack(e)
    def spread(i, j, src):
        for n in range(2):
            part = pl.ds(n * CH, CH)
            cp = remote(src.at[:, part], rows.at[c, par, j, :, part], n_s.at[n, i], n_r.at[n, j], near[n])
            cp.start()
            sends.append(cp)
        cp = remote(src, rows.at[c, par, j], c_s.at[0, i], c_r.at[0, j], twin)
        cp.start()
        sends.append(cp)

    spread(7, e, sendb.at[e])
    own = pltpu.make_async_copy(sendb.at[e], rows.at[c, par, e], lsem.at[5])
    own.start()

    for m in range(NP):
        for n, (src, dst) in enumerate((
            (wd_hbm.at[:, pl.ds(pl.multiple_of((2 * m + 1 - c) * CH, CH), CH)], wdx.at[m]),
            (wg_hbm.at[pl.ds(pl.multiple_of((2 * m + c) * CH, CH), CH)], wgx.at[m]),
            (wu_hbm.at[pl.ds(pl.multiple_of((2 * m + c) * CH, CH), CH)], wux.at[m]),
        )):
            cp = remote(src, dst, ws_s.at[n, m], ws_r.at[n, m], twin)
            cp.start()
            sends.append(cp)

    expand = (iota((T, NE * BLK), 0) == iota((T, NE * BLK), 1) // BLK).astype(F32).astype(BF16)
    weight_t = weight.T
    w_hi = weight_t.astype(BF16)
    w_lo = (weight_t - w_hi.astype(F32)).astype(BF16)
    inner = (iota((T, NE * BLK), 1) % BLK).astype(F32)
    slots_all = nn(slot.T.astype(BF16), expand)
    out_hit = slots_all == inner
    tmat[0:T] = jnp.where(out_hit, nn(w_hi, expand), 0.0).astype(BF16)
    tmat[T:2 * T] = jnp.where(out_hit, nn(w_lo, expand), 0.0).astype(BF16)
    tmat[2 * T:3 * T] = (slots_all == inner - CAP).astype(F32).astype(BF16)

    for i, step in enumerate(PLANE):
        j = plane((4 - step[0], step[1]))
        here = rows.at[c, par, j]
        remote(here, here, d_s.at[i], d_r.at[j], (d, j)).wait_recv()
        spread(i, j, here)
    own.wait()
    for cp in loads[2:]:
        cp.wait()

    def x_rows(cc, pp):
        return rows[cc, pp, :, 0:SLAB, :].reshape(NE * SLAB, QD)

    def e_rows(cc, pp):
        return rows[cc, pp, :, BLK - SLAB:BLK, :].reshape(NE * SLAB, QD)

    def products(cc, pp):
        at = pl.ds(pl.multiple_of(cc * HD + pp * QD, QD), QD)
        xs = x_rows(cc, pp)
        return nn(xs, wg[at, :]), nn(xs, wu[at, :]), nt(e_rows(cc, pp), wd[:, at])

    def first(a):
        return a.reshape(NE, SLAB, W)[:, 0:CAP].reshape(NE * CAP, W)

    def last(a):
        return a.reshape(NE, SLAB, W)[:, SLAB - CAP:].reshape(NE * CAP, W)

    sum3 = products(c, par)
    for i, step in enumerate(((0, 0),) + PLANE):
        j = plane((4 - step[0], step[1]))
        there = rows.at[c, 1 - par, j]
        for n in range(2):
            part = there.at[:, pl.ds(n * CH, CH)]
            remote(part, part, n_s.at[n, i], n_r.at[n, j], near[n]).wait_recv()
        cp = remote(there, there, c_s.at[1, i], c_r.at[1, j], twin)
        cp.start()
        sends.append(cp)
    for n, pp in enumerate((par, 1 - par)):
        for i, step in enumerate(((0, 0),) + PLANE):
            j = plane((4 - step[0], step[1]))
            there = rows.at[1 - c, pp, j]
            remote(there, there, c_s.at[n, i], c_r.at[n, j], twin).wait_recv()
        if n == 0:
            sum3 = [u + v for u, v in zip(sum3, products(1 - c, par))]
            sum3 = [u + v for u, v in zip(sum3, products(c, 1 - par))]
        else:
            sum3 = [u + v for u, v in zip(sum3, products(1 - c, 1 - par))]
    gate, up, hgrad = first(sum3[0]), first(sum3[1]), last(sum3[2])
    sig = jax.nn.sigmoid(gate)
    active = gate * sig
    hidden = (active * up).astype(BF16)
    gate_grad = (hgrad * up * sig * (1.0 + gate * (1.0 - sig))).astype(BF16)
    up_grad = (hgrad * active).astype(BF16)
    acts[0] = hidden
    acts[1] = gate_grad
    acts[2] = up_grad
    xact = remote(acts, actx, x_s, x_r, twin)
    xact.start()
    hid32 = hidden.astype(F32)
    dots = jnp.sum(hid32 * hgrad, axis=1, keepdims=True)
    gsend[...] = jnp.broadcast_to(dots, (NE * CAP, T)).reshape(NE, CAP, T)
    for i, step in enumerate(PLANE):
        j = plane(step)
        cp = remote(gsend.at[j], grecv.at[e], g_s.at[i], g_r.at[e], (d, j))
        cp.start()
        sends.append(cp)
    grecv[e] = gsend[e]
    for n in range(3):
        for m in range(NP):
            cp = remote(
                (wdx, wgx, wux)[n].at[m], (wdx, wgx, wux)[n].at[m], ws_s.at[n, m], ws_r.at[n, m], twin
            )
            cp.wait_recv()
    xact.wait_recv()

    for s in range(NP):
        m = (z // 2 + FAR[s]) % NP
        oc = pl.multiple_of((2 * m + c) * CH, CH)
        tcol = pl.multiple_of((2 * m + 1 - c) * CH, CH)
        out = nn(acts[0], wd[:, pl.ds(oc, CH)]) + nn(actx[0], wdx[m])
        back = (
            nt(acts[1], wg[pl.ds(tcol, CH), :]) + nt(acts[2], wu[pl.ds(tcol, CH), :])
            + nt(actx[1], wgx[m]) + nt(actx[2], wux[m])
        )
        both = jnp.concatenate([out.reshape(NE, CAP, CH), back.reshape(NE, CAP, CH)], axis=1)
        rsend[s] = both.astype(BF16)
        for i, step in enumerate(PLANE):
            j = plane(step)
            cp = remote(rsend.at[s, j], rrecv.at[s, e], r_s.at[s, i], r_r.at[s, e], (d, j))
            cp.start()
            sends.append(cp)
        rrecv[s, e] = rsend[s, e]

    for step in PLANE:
        j = plane((4 - step[0], step[1]))
        remote(gsend.at[j], grecv.at[j], g_s.at[0], g_r.at[j], (d, j)).wait_recv()
    q = iota((NE * CAP, T), 0).astype(F32)
    values = grecv[...].reshape(NE * CAP, T)

    def gathered(pick, c_row):
        place = jnp.sum(jnp.where(pick, deep.astype(F32) * CAP + rank, 0.0), axis=0, keepdims=True)
        return jnp.sum(jnp.where(q == place, values, 0.0), axis=0, keepdims=True) / c_row

    sub = iota((8, T), 0)
    gzrecv[z] = jnp.where(
        sub == 0, gathered(pick0, comb[0:1]), jnp.where(sub == 1, gathered(pick1, comb[1:2]), 0.0)
    )
    for k in range(1, NZ):
        cp = remote(gzrecv.at[z], gzrecv.at[z], gz_s.at[k], gz_r.at[z], zdev(at_z(k)))
        cp.start()
        sends.append(cp)

    def padded(a, lead):
        a = a.astype(F32).reshape(NE, CAP, W)
        zero = jnp.zeros((NE, SLAB - CAP, W), F32)
        a = jnp.concatenate([a, zero] if lead else [zero, a], axis=1)
        return a.reshape(NE * SLAB, W).astype(BF16)

    hid_pad = padded(acts[0], False)
    pair_pad = jnp.concatenate([padded(acts[1], True), padded(acts[2], True)], axis=1)
    stores = []

    def weight_grads(k):
        at = k * QD
        both = tn(x_rows(k // 2, k % 2), pair_pad)
        og[at:at + QD] = both[:, 0:W].astype(BF16)
        ou[at:at + QD] = both[:, W:2 * W].astype(BF16)
        od[:, at:at + QD] = tn(hid_pad, e_rows(k // 2, k % 2)).astype(BF16)
        for n, (src, dst) in enumerate((
            (og.at[pl.ds(at, QD)], gg_hbm.at[pl.ds(at, QD)]),
            (ou.at[pl.ds(at, QD)], gu_hbm.at[pl.ds(at, QD)]),
            (od.at[:, pl.ds(at, QD)], gd_hbm.at[:, pl.ds(at, QD)]),
        )):
            cp = pltpu.make_async_copy(src, dst, osem.at[n, k])
            cp.start()
            stores.append(cp)

    mine = par == c
    windows = [pl.ds(pl.multiple_of(T * hh, T), 2 * T) for hh in (h, 1 - h)]
    for s in range(NP):
        weight_grads(s)
        for step in PLANE:
            j = plane((4 - step[0], step[1]))
            remote(rsend.at[s, j], rrecv.at[s, j], r_s.at[s, 0], r_r.at[s, j], (d, j)).wait_recv()
        m = (z // 2 + FAR[s]) % NP
        sums = nn(tmat[...], rrecv[s].reshape(NE * BLK, CH))
        mix = sums[0:T] + sums[T:2 * T]
        back = sums[2 * T:3 * T]
        if s < NP - 1:
            zsend[s, 0] = mix.astype(BF16)
            zsend[s, 1] = back.astype(BF16)
            for n in range(2):
                to = 2 * m + (c if n == 0 else 1 - c)
                cp = remote(zsend.at[s, n], zrecv.at[z], z_s.at[s, n], z_r.at[z], zdev(to))
                cp.start()
                sends.append(cp)
        else:
            zsend[s, 0] = jnp.where(mine, back, mix).astype(BF16)
            for n, (src, dev) in enumerate((
                (zsend.at[s, 0, :, windows[0]], zdev(mate)),
                (zsend.at[s, 0, :, windows[1]], mate_over),
            )):
                cp = remote(src, yrecv.at[n], y_s.at[n], y_r.at[n], dev)
                cp.start()
                sends.append(cp)
            total = jnp.where(mine, mix, back)
    for k in FAR[:NP - 1]:
        for n in range(2):
            zz = 2 * ((z // 2 + NP - k) % NP) + n
            remote(zsend.at[0, 0], zrecv.at[zz], z_s.at[0, 0], z_r.at[zz], zdev(zz)).wait_recv()
            total = total + zrecv[zz].astype(F32)
    ysend[...] = total.astype(BF16)
    yc = remote(ysend.at[:, windows[1]], yrecv.at[2], y_s.at[2], y_r.at[2], over)
    yc.start()
    for k in range(1, NZ):
        zz = at_z(k)
        remote(gzrecv.at[zz], gzrecv.at[zz], gz_s.at[k], gz_r.at[zz], zdev(zz)).wait_recv()
    gc_sum = gzrecv[0]
    for k in range(1, NZ):
        gc_sum = gc_sum + gzrecv[k]
    gycs[0] = gc_sum
    gy = remote(gycs.at[0], gycs.at[1], p_s.at[0], p_r.at[0], over)
    gy.start()
    gy.wait_recv()
    gc_sum = gc_sum + gycs[1]
    gycs[2] = gc_sum
    gx = remote(gycs.at[2], gycs.at[3], p_s.at[1], p_r.at[1], twin)
    gx.start()
    for n in range(3):
        remote(yrecv.at[n], yrecv.at[n], y_s.at[n], y_r.at[n], over).wait_recv()
    window = jnp.where(h == 0, total[:, 0:2 * T], total[:, T:3 * T])
    window = window + yrecv[0].astype(F32) + yrecv[1].astype(F32) + yrecv[2].astype(F32)
    final = window.astype(BF16)
    fsend[...] = final
    fc = remote(fsend, frecv, p_s.at[2], p_r.at[2], twin)
    fc.start()
    shift = 64 * h + 96 * c
    pick = (iota((T, 2 * T), 1) == iota((T, 2 * T), 0) + shift).astype(F32).astype(BF16)
    gx.wait_recv()
    gc_sum = gc_sum + gycs[3]
    gcomb_ref[...] = gc_sum[0:2]
    a = nt(pick, final)
    fc.wait_recv()
    b = nt(pick, frecv[...])
    mixed_ref[...] = jnp.where(mine, a, b)[0:96].astype(BF16)
    gtok_ref[...] = jnp.where(mine, b, a)[0:96].astype(BF16)

    for cp in sends:
        cp.wait_send()
    for cp in (xact, gy, yc, gx, fc):
        cp.wait_send()
    for cp in stores:
        cp.wait()


def settle_kernel(*refs):
    sources, targets, held, came, went = refs[0:6], refs[6:12], refs[12:18], refs[18], refs[19]
    moves = []
    for i in range(6):
        rows = sources[i].shape[0]
        parts = 4 if rows * sources[i].shape[1] > T * T else 1
        for k in range(parts):
            cut = pl.ds(k * (rows // parts), rows // parts)
            moves.append((i, k, cut))
    ins = [pltpu.make_async_copy(sources[i].at[cut], held[i].at[cut], came.at[i, k]) for i, k, cut in moves]
    outs = [pltpu.make_async_copy(held[i].at[cut], targets[i].at[cut], went.at[i, k]) for i, k, cut in moves]
    for cp in ins:
        cp.start()
    for come, go in zip(ins, outs):
        come.wait()
        go.start()
    for cp in outs:
        cp.wait()


def settle(*arrays):
    any_spec = pl.BlockSpec(memory_space=pl.ANY)
    return pl.pallas_call(
        settle_kernel,
        out_shape=tuple(jax.ShapeDtypeStruct(a.shape, a.dtype) for a in arrays),
        in_specs=[any_spec] * 6,
        out_specs=(any_spec,) * 6,
        scratch_shapes=[pltpu.VMEM(a.shape, a.dtype) for a in arrays]
        + [pltpu.SemaphoreType.DMA((6, 4)), pltpu.SemaphoreType.DMA((6, 4))],
        compiler_params=pltpu.CompilerParams(vmem_limit_bytes=60 * 1024 * 1024),
        name="settle",
    )(*arrays)


def local(tokens, expert_ids, combine, cotangent, w_gate, w_up, w_down):
    any_spec = pl.BlockSpec(memory_space=pl.ANY)
    vmem = pl.BlockSpec(memory_space=pltpu.VMEM)
    dma = pltpu.SemaphoreType.DMA
    mixed, gtok, gcomb, gg, gu, gd = pl.pallas_call(
        kernel,
        out_shape=(
            jax.ShapeDtypeStruct((96, T), BF16),
            jax.ShapeDtypeStruct((96, T), BF16),
            jax.ShapeDtypeStruct((2, T), F32),
            jax.ShapeDtypeStruct((D, W), BF16),
            jax.ShapeDtypeStruct((D, W), BF16),
            jax.ShapeDtypeStruct((W, D), BF16),
        ),
        in_specs=[any_spec, vmem, vmem, any_spec, any_spec, any_spec, any_spec],
        out_specs=(vmem, vmem, vmem, any_spec, any_spec, any_spec),
        scratch_shapes=[
            pltpu.VMEM((2 * T, QD), BF16),
            pltpu.VMEM((D, W), BF16),
            pltpu.VMEM((D, W), BF16),
            pltpu.VMEM((W, D), BF16),
            pltpu.VMEM((NP, CH, W), BF16),
            pltpu.VMEM((NP, CH, W), BF16),
            pltpu.VMEM((NP, W, CH), BF16),
            pltpu.VMEM((NE, 2 * T), F32),
            pltpu.VMEM((NE, 2 * T), F32),
            pltpu.VMEM((NE, BLK, QD), BF16),
            pltpu.VMEM((2, 2, NE, BLK, QD), BF16),
            pltpu.VMEM((3, NE * CAP, W), BF16),
            pltpu.VMEM((3, NE * CAP, W), BF16),
            pltpu.VMEM((NE, CAP, T), F32),
            pltpu.VMEM((NE, CAP, T), F32),
            pltpu.VMEM((3 * T, NE * BLK), BF16),
            pltpu.VMEM((NP, NE, BLK, CH), BF16),
            pltpu.VMEM((NP, NE, BLK, CH), BF16),
            pltpu.VMEM((NP, 2, T, CH), BF16),
            pltpu.VMEM((NZ, T, CH), BF16),
            pltpu.VMEM((NZ, 8, T), F32),
            pltpu.VMEM((T, CH), BF16),
            pltpu.VMEM((3, T, 2 * T), BF16),
            pltpu.VMEM((4, 8, T), F32),
            pltpu.VMEM((T, 2 * T), BF16),
            pltpu.VMEM((T, 2 * T), BF16),
            pltpu.VMEM((D, W), BF16),
            pltpu.VMEM((D, W), BF16),
            pltpu.VMEM((W, D), BF16),
            dma((6,)),
            dma((3, 4)),
            dma((3, NP)),
            dma((3, NP)),
            dma((7,)),
            dma((NE,)),
            dma((2, 8)),
            dma((2, NE)),
            dma((2, 8)),
            dma((2, NE)),
            dma,
            dma,
            dma((7,)),
            dma((NE,)),
            dma((NP, 7)),
            dma((NP, NE)),
            dma((NP, 2)),
            dma((NZ,)),
            dma((NZ,)),
            dma((NZ,)),
            dma((3,)),
            dma((3,)),
            dma((3,)),
            dma((3,)),
        ],
        compiler_params=pltpu.CompilerParams(
            collective_id=0, has_side_effects=True, vmem_limit_bytes=60 * 1024 * 1024
        ),
        name="moe_layer",
    )(tokens, expert_ids.T, combine.T, cotangent, w_gate[0], w_up[0], w_down[0])
    mixed, gtok, gcomb, gg, gu, gd = settle(mixed, gtok, gcomb, gg, gu, gd)
    return mixed.T, gtok.T, gcomb.T, gg[None], gu[None], gd[None]


def solution(mesh):
    in_specs = (
        P("expert", None),
        P("expert", None),
        P("expert", None),
        P("expert", None),
        P("expert", None, "dp"),
        P("expert", None, "dp"),
        P("expert", "dp", None),
    )
    out_specs = (
        P("expert", "dp"),
        P("expert", "dp"),
        P("expert", None),
        P("expert", None, "dp"),
        P("expert", None, "dp"),
        P("expert", "dp", None),
    )
    return jax.shard_map(local, mesh=mesh, in_specs=in_specs, out_specs=out_specs, check_vma=False)
```

```python
import jax
import jax.numpy as jnp
from jax import lax
from jax.experimental import pallas as pl
from jax.experimental.pallas import tpu as pltpu
from jax.sharding import PartitionSpec as P

MESH = pl.DeviceIdType.MESH
F32 = jnp.float32
BF16 = jnp.bfloat16

T = 128
D = 3072
HD = 1536
QD = 768
CAP = 40
BLK = 2 * CAP
SLAB = 48
NE = 8
NZ = 8
W = 256
CH = 384
NP = 4

FAR = ((4, 1), (2, 5), (6, 3), (0, 7))

PLANE = ((2, 1), (1, 1), (3, 1), (2, 0), (0, 1), (1, 0), (3, 0))


def nn(a, b):
    return lax.dot_general(a, b, (((1,), (0,)), ((), ())), preferred_element_type=F32)


def nt(a, b):
    return lax.dot_general(a, b, (((1,), (1,)), ((), ())), preferred_element_type=F32)


def tn(a, b):
    return lax.dot_general(a, b, (((0,), (0,)), ((), ())), preferred_element_type=F32)


def iota(shape, axis):
    return lax.broadcasted_iota(jnp.int32, shape, axis)


def kernel(
    tok_hbm, ids_ref, comb_ref, cot_hbm, wg_hbm, wu_hbm, wd_hbm,
    mixed_ref, gtok_ref, gcomb_ref, og, ou, od,
    tc, wg, wu, wd, wgx, wux, wdx, slt, cwt, sendb, rows, acts, actx,
    gsend, grecv, tmat, rsend, rrecv, zsend, zrecv, gzrecv, ysend, yrecv, gycs,
    fsend, frecv,
    lsem, ws_s, ws_r, d_s, d_r, n_s, n_r, c_s, c_r, x_s, x_r, g_s, g_r, r_s, r_r,
    z_s, z_r, gz_s, gz_r, y_s, y_r, p_s, p_r,
):
    d = lax.axis_index("dp")
    e = lax.axis_index("expert")
    z, h, c = d // 4, (d // 2) % 2, d % 2
    yl, x = e // 4, e % 4
    twin = (z * 4 + h * 2 + (1 - c), e)
    over = (z * 4 + (1 - h) * 2 + c, e)

    def plane(step):
        return ((yl + step[1]) % 2) * 4 + (x + step[0]) % 4

    def at_z(k):
        return (z + k) % NZ

    def zdev(zz):
        return (zz * 4 + h * 2 + c, e)

    def remote(src, dst, ssem, rsem, dev):
        return pltpu.make_async_remote_copy(
            src_ref=src, dst_ref=dst, send_sem=ssem, recv_sem=rsem, device_id=dev, device_id_type=MESH
        )

    par = z % 2
    quarter = pl.multiple_of(c * HD + par * QD, QD)
    mine = par == c
    below = at_z(NZ - 1)
    below_over = (below * 4 + (1 - h) * 2 + c, e)
    above_over = (at_z(1) * 4 + (1 - h) * 2 + c, e)
    near = (zdev(z + 1 - 2 * par), zdev((z + 2 * par + NZ - 1) % NZ))

    loads = [
        pltpu.make_async_copy(tok_hbm.at[:, pl.ds(quarter, QD)], tc.at[pl.ds(0, T)], lsem.at[0]),
        pltpu.make_async_copy(cot_hbm.at[:, pl.ds(quarter, QD)], tc.at[pl.ds(T, T)], lsem.at[1]),
        pltpu.make_async_copy(wg_hbm, wg, lsem.at[2]),
        pltpu.make_async_copy(wu_hbm, wu, lsem.at[3]),
        pltpu.make_async_copy(wd_hbm, wd, lsem.at[4]),
    ]
    for cp in loads:
        cp.start()

    barrier = pltpu.get_barrier_semaphore()
    for step in PLANE:
        pl.semaphore_signal(barrier, inc=1, device_id=(d, plane(step)), device_id_type=MESH)
    for k in range(1, NZ):
        pl.semaphore_signal(barrier, inc=1, device_id=zdev(at_z(k)), device_id_type=MESH)
    pl.semaphore_signal(barrier, inc=1, device_id=twin, device_id_type=MESH)
    pl.semaphore_signal(barrier, inc=1, device_id=over, device_id_type=MESH)
    pl.semaphore_signal(barrier, inc=1, device_id=below_over, device_id_type=MESH)
    pl.semaphore_signal(barrier, inc=1, device_id=above_over, device_id_type=MESH)

    deep = iota((T, T), 0)
    lane = iota((T, T), 1)
    ids = ids_ref[...]
    comb = comb_ref[...]
    pick0 = deep == ids[0:1]
    pick1 = deep == ids[1:2]
    chosen = jnp.logical_or(pick0, pick1)
    earlier = (deep < lane).astype(F32).astype(BF16)
    rank = nn(chosen.astype(F32).astype(BF16), earlier)
    slot = jnp.where(chosen, rank, -128.0)
    weight = jnp.where(pick0, comb[0:1], 0.0) + jnp.where(pick1, comb[1:2], 0.0)
    slt[...] = jnp.concatenate([slot[0:NE], slot[0:NE]], axis=1)
    cwt[...] = jnp.concatenate([jnp.ones((NE, T), F32), weight[0:NE]], axis=1)

    loads[0].wait()
    loads[1].wait()

    def pack(j):
        slots = slt[pl.ds(j, 1), :]
        weights = cwt[pl.ds(j, 1), :]
        row = iota((BLK, 2 * T), 0)
        col = iota((BLK, 2 * T), 1)
        want = jnp.where(col < T, row, row - CAP).astype(F32)
        hit = want == slots
        scale = jnp.sum(jnp.where(hit, weights, 0.0), axis=1, keepdims=True)
        block = nn(hit.astype(F32).astype(BF16), tc[...])
        sendb[j] = (block * scale).astype(BF16)

    sends = []
    for i, step in enumerate(PLANE):
        j = plane(step)
        pack(j)
        if i == 0:
            pl.semaphore_wait(barrier, len(PLANE) + NZ - 1 + 4)
        cp = remote(sendb.at[j], rows.at[c, par, e], d_s.at[i], d_r.at[e], (d, j))
        cp.start()
        sends.append(cp)
    pack(e)
    def spread(i, j, src):
        for n in range(2):
            part = pl.ds(n * CH, CH)
            cp = remote(src.at[:, part], rows.at[c, par, j, :, part], n_s.at[n, i], n_r.at[n, j], near[n])
            cp.start()
            sends.append(cp)
        cp = remote(src, rows.at[c, par, j], c_s.at[0, i], c_r.at[0, j], twin)
        cp.start()
        sends.append(cp)

    spread(7, e, sendb.at[e])
    own = pltpu.make_async_copy(sendb.at[e], rows.at[c, par, e], lsem.at[5])
    own.start()

    for m in range(NP):
        for n, (src, dst) in enumerate((
            (wd_hbm.at[:, pl.ds(pl.multiple_of((2 * m + 1 - c) * CH, CH), CH)], wdx.at[m]),
            (wg_hbm.at[pl.ds(pl.multiple_of((2 * m + c) * CH, CH), CH)], wgx.at[m]),
            (wu_hbm.at[pl.ds(pl.multiple_of((2 * m + c) * CH, CH), CH)], wux.at[m]),
        )):
            cp = remote(src, dst, ws_s.at[n, m], ws_r.at[n, m], twin)
            cp.start()
            sends.append(cp)

    expand = (iota((T, NE * BLK), 0) == iota((T, NE * BLK), 1) // BLK).astype(F32).astype(BF16)
    weight_t = weight.T
    w_hi = weight_t.astype(BF16)
    w_lo = (weight_t - w_hi.astype(F32)).astype(BF16)
    inner = (iota((T, NE * BLK), 1) % BLK).astype(F32)
    slots_all = nn(slot.T.astype(BF16), expand)
    out_hit = slots_all == inner
    tmat[0:T] = jnp.where(out_hit, nn(w_hi, expand), 0.0).astype(BF16)
    tmat[T:2 * T] = jnp.where(out_hit, nn(w_lo, expand), 0.0).astype(BF16)
    tmat[2 * T:3 * T] = (slots_all == inner - CAP).astype(F32).astype(BF16)

    for i, step in enumerate(PLANE):
        j = plane((4 - step[0], step[1]))
        here = rows.at[c, par, j]
        remote(here, here, d_s.at[i], d_r.at[j], (d, j)).wait_recv()
        spread(i, j, here)
    own.wait()
    for cp in loads[2:]:
        cp.wait()

    def x_rows(cc, pp):
        return rows[cc, pp, :, 0:SLAB, :].reshape(NE * SLAB, QD)

    def e_rows(cc, pp):
        return rows[cc, pp, :, BLK - SLAB:BLK, :].reshape(NE * SLAB, QD)

    def products(cc, pp):
        at = pl.ds(pl.multiple_of(cc * HD + pp * QD, QD), QD)
        xs = x_rows(cc, pp)
        return nn(xs, wg[at, :]), nn(xs, wu[at, :]), nt(e_rows(cc, pp), wd[:, at])

    def first(a):
        return a.reshape(NE, SLAB, W)[:, 0:CAP].reshape(NE * CAP, W)

    def last(a):
        return a.reshape(NE, SLAB, W)[:, SLAB - CAP:].reshape(NE * CAP, W)

    sum3 = products(c, par)
    for i, step in enumerate(((0, 0),) + PLANE):
        j = plane((4 - step[0], step[1]))
        there = rows.at[c, 1 - par, j]
        for n in range(2):
            part = there.at[:, pl.ds(n * CH, CH)]
            remote(part, part, n_s.at[n, i], n_r.at[n, j], near[n]).wait_recv()
        cp = remote(there, there, c_s.at[1, i], c_r.at[1, j], twin)
        cp.start()
        sends.append(cp)
    for n, pp in enumerate((par, 1 - par)):
        for i, step in enumerate(((0, 0),) + PLANE):
            j = plane((4 - step[0], step[1]))
            there = rows.at[1 - c, pp, j]
            remote(there, there, c_s.at[n, i], c_r.at[n, j], twin).wait_recv()
        if n == 0:
            sum3 = [u + v for u, v in zip(sum3, products(1 - c, par))]
            sum3 = [u + v for u, v in zip(sum3, products(c, 1 - par))]
        else:
            sum3 = [u + v for u, v in zip(sum3, products(1 - c, 1 - par))]
    gate, up, hgrad = first(sum3[0]), first(sum3[1]), last(sum3[2])
    sig = jax.nn.sigmoid(gate)
    active = gate * sig
    hidden = (active * up).astype(BF16)
    gate_grad = (hgrad * up * sig * (1.0 + gate * (1.0 - sig))).astype(BF16)
    up_grad = (hgrad * active).astype(BF16)
    acts[0] = hidden
    acts[1] = gate_grad
    acts[2] = up_grad
    xact = remote(acts, actx, x_s, x_r, twin)
    xact.start()
    hid32 = hidden.astype(F32)
    dots = jnp.sum(hid32 * hgrad, axis=1, keepdims=True)
    gsend[...] = jnp.broadcast_to(dots, (NE * CAP, T)).reshape(NE, CAP, T)
    for i, step in enumerate(PLANE):
        j = plane(step)
        cp = remote(gsend.at[j], grecv.at[e], g_s.at[i], g_r.at[e], (d, j))
        cp.start()
        sends.append(cp)
    grecv[e] = gsend[e]

    def targets(s):
        even, odd = at_z(FAR[s][0]), at_z(FAR[s][1])
        return jnp.where(mine, even, odd), jnp.where(mine, odd, even)

    def own_sums(s):
        to_out, to_back = targets(s)
        oc = pl.multiple_of(to_out * CH, CH)
        tcol = pl.multiple_of(to_back * CH, CH)
        out = nn(acts[0], wd[:, pl.ds(oc, CH)])
        return out, nt(acts[1], wg[pl.ds(tcol, CH), :]) + nt(acts[2], wu[pl.ds(tcol, CH), :])

    start = own_sums(0)
    for n in range(3):
        for m in range(NP):
            there = (wdx, wgx, wux)[n].at[m]
            remote(there, there, ws_s.at[n, m], ws_r.at[n, m], twin).wait_recv()
    xact.wait_recv()

    for s in range(NP):
        to_out, to_back = targets(s)
        out, back = own_sums(s) if s else start
        out = out + nn(actx[0], wdx[to_out // 2])
        back = back + nt(actx[1], wgx[to_back // 2]) + nt(actx[2], wux[to_back // 2])
        both = jnp.concatenate([out.reshape(NE, CAP, CH), back.reshape(NE, CAP, CH)], axis=1)
        rsend[s] = both.astype(BF16)
        for i, step in enumerate(PLANE):
            j = plane(step)
            cp = remote(rsend.at[s, j], rrecv.at[s, e], r_s.at[s, i], r_r.at[s, e], (d, j))
            cp.start()
            sends.append(cp)
        rrecv[s, e] = rsend[s, e]

    for step in PLANE:
        j = plane((4 - step[0], step[1]))
        remote(gsend.at[j], grecv.at[j], g_s.at[0], g_r.at[j], (d, j)).wait_recv()
    q = iota((NE * CAP, T), 0).astype(F32)
    values = grecv[...].reshape(NE * CAP, T)

    def gathered(pick, c_row):
        place = jnp.sum(jnp.where(pick, deep.astype(F32) * CAP + rank, 0.0), axis=0, keepdims=True)
        return jnp.sum(jnp.where(q == place, values, 0.0), axis=0, keepdims=True) / c_row

    sub = iota((8, T), 0)
    gzrecv[z] = jnp.where(
        sub == 0, gathered(pick0, comb[0:1]), jnp.where(sub == 1, gathered(pick1, comb[1:2]), 0.0)
    )
    for k in range(1, NZ):
        cp = remote(gzrecv.at[z], gzrecv.at[z], gz_s.at[k], gz_r.at[z], zdev(at_z(k)))
        cp.start()
        sends.append(cp)

    def padded(a, lead):
        a = a.astype(F32).reshape(NE, CAP, W)
        zero = jnp.zeros((NE, SLAB - CAP, W), F32)
        a = jnp.concatenate([a, zero] if lead else [zero, a], axis=1)
        return a.reshape(NE * SLAB, W).astype(BF16)

    hid_pad = padded(acts[0], False)
    pair_pad = jnp.concatenate([padded(acts[1], True), padded(acts[2], True)], axis=1)
    def weight_grads(k):
        at = k * QD
        both = tn(x_rows(k // 2, k % 2), pair_pad)
        og[at:at + QD] = both[:, 0:W].astype(BF16)
        ou[at:at + QD] = both[:, W:2 * W].astype(BF16)
        od[:, at:at + QD] = tn(hid_pad, e_rows(k // 2, k % 2)).astype(BF16)

    windows = [pl.ds(pl.multiple_of(T * hh, T), 2 * T) for hh in (h, 1 - h)]
    for s in range(NP):
        weight_grads(s)
        for step in PLANE:
            j = plane((4 - step[0], step[1]))
            remote(rsend.at[s, j], rrecv.at[s, j], r_s.at[s, 0], r_r.at[s, j], (d, j)).wait_recv()
        sums = nn(tmat[...], rrecv[s].reshape(NE * BLK, CH))
        mix = sums[0:T] + sums[T:2 * T]
        back = sums[2 * T:3 * T]
        if s < NP - 1:
            zsend[s, 0] = mix.astype(BF16)
            zsend[s, 1] = back.astype(BF16)
            for n in range(2):
                cp = remote(zsend.at[s, n], zrecv.at[z], z_s.at[s, n], z_r.at[z], zdev(targets(s)[n]))
                cp.start()
                sends.append(cp)
        else:
            zsend[s, 0] = jnp.where(mine, back, mix).astype(BF16)
            for n, (src, dev) in enumerate((
                (zsend.at[s, 0, :, windows[0]], zdev(below)),
                (zsend.at[s, 0, :, windows[1]], below_over),
            )):
                cp = remote(src, yrecv.at[n], y_s.at[n], y_r.at[n], dev)
                cp.start()
                sends.append(cp)
            total = jnp.where(mine, mix, back)
    for k in FAR[:NP - 1]:
        for n in range(2):
            zz = at_z(NZ - k[n])
            remote(zsend.at[0, 0], zrecv.at[zz], z_s.at[0, 0], z_r.at[zz], zdev(zz)).wait_recv()
            total = total + zrecv[zz].astype(F32)
    ysend[...] = total.astype(BF16)
    yc = remote(ysend.at[:, windows[1]], yrecv.at[2], y_s.at[2], y_r.at[2], over)
    yc.start()
    for k in range(1, NZ):
        zz = at_z(k)
        remote(gzrecv.at[zz], gzrecv.at[zz], gz_s.at[k], gz_r.at[zz], zdev(zz)).wait_recv()
    gc_sum = gzrecv[0]
    for k in range(1, NZ):
        gc_sum = gc_sum + gzrecv[k]
    gycs[0] = gc_sum
    gy = remote(gycs.at[0], gycs.at[1], p_s.at[0], p_r.at[0], over)
    gy.start()
    gy.wait_recv()
    gc_sum = gc_sum + gycs[1]
    gycs[2] = gc_sum
    gx = remote(gycs.at[2], gycs.at[3], p_s.at[1], p_r.at[1], twin)
    gx.start()
    for n in range(3):
        remote(yrecv.at[n], yrecv.at[n], y_s.at[n], y_r.at[n], over).wait_recv()
    window = jnp.where(h == 0, total[:, 0:2 * T], total[:, T:3 * T])
    window = window + yrecv[0].astype(F32) + yrecv[1].astype(F32) + yrecv[2].astype(F32)
    final = window.astype(BF16)
    fsend[...] = final
    fc = remote(fsend, frecv, p_s.at[2], p_r.at[2], twin)
    fc.start()
    shift = 64 * h + 96 * c
    pick = (iota((T, 2 * T), 1) == iota((T, 2 * T), 0) + shift).astype(F32).astype(BF16)
    gx.wait_recv()
    gc_sum = gc_sum + gycs[3]
    gcomb_ref[...] = gc_sum[0:2]
    a = nt(pick, final)
    fc.wait_recv()
    b = nt(pick, frecv[...])
    mixed_ref[...] = jnp.where(mine, a, b)[0:96].astype(BF16)
    gtok_ref[...] = jnp.where(mine, b, a)[0:96].astype(BF16)

    for cp in sends:
        cp.wait_send()
    for cp in (xact, gy, yc, gx, fc):
        cp.wait_send()


def settle_kernel(*refs):
    copies = [pltpu.make_async_copy(refs[i], refs[6 + i], refs[12].at[i]) for i in range(6)]
    for cp in copies:
        cp.start()
    for cp in copies:
        cp.wait()


def settle(*arrays):
    any_spec = pl.BlockSpec(memory_space=pl.ANY)
    return pl.pallas_call(
        settle_kernel,
        out_shape=tuple(jax.ShapeDtypeStruct(a.shape, a.dtype) for a in arrays),
        in_specs=[any_spec] * 6,
        out_specs=(any_spec,) * 6,
        scratch_shapes=[pltpu.SemaphoreType.DMA((6,))],
        compiler_params=pltpu.CompilerParams(vmem_limit_bytes=16 * 1024 * 1024),
        name="settle",
    )(*arrays)


def local(tokens, expert_ids, combine, cotangent, w_gate, w_up, w_down):
    any_spec = pl.BlockSpec(memory_space=pl.ANY)
    vmem = pl.BlockSpec(memory_space=pltpu.VMEM)
    dma = pltpu.SemaphoreType.DMA
    mixed, gtok, gcomb, gg, gu, gd = pl.pallas_call(
        kernel,
        out_shape=(
            pltpu.VMEM((96, T), BF16),
            pltpu.VMEM((96, T), BF16),
            pltpu.VMEM((2, T), F32),
            pltpu.VMEM((D, W), BF16),
            pltpu.VMEM((D, W), BF16),
            pltpu.VMEM((W, D), BF16),
        ),
        in_specs=[any_spec, vmem, vmem, any_spec, any_spec, any_spec, any_spec],
        out_specs=(vmem,) * 6,
        scratch_shapes=[
            pltpu.VMEM((2 * T, QD), BF16),
            pltpu.VMEM((D, W), BF16),
            pltpu.VMEM((D, W), BF16),
            pltpu.VMEM((W, D), BF16),
            pltpu.VMEM((NP, CH, W), BF16),
            pltpu.VMEM((NP, CH, W), BF16),
            pltpu.VMEM((NP, W, CH), BF16),
            pltpu.VMEM((NE, 2 * T), F32),
            pltpu.VMEM((NE, 2 * T), F32),
            pltpu.VMEM((NE, BLK, QD), BF16),
            pltpu.VMEM((2, 2, NE, BLK, QD), BF16),
            pltpu.VMEM((3, NE * CAP, W), BF16),
            pltpu.VMEM((3, NE * CAP, W), BF16),
            pltpu.VMEM((NE, CAP, T), F32),
            pltpu.VMEM((NE, CAP, T), F32),
            pltpu.VMEM((3 * T, NE * BLK), BF16),
            pltpu.VMEM((NP, NE, BLK, CH), BF16),
            pltpu.VMEM((NP, NE, BLK, CH), BF16),
            pltpu.VMEM((NP, 2, T, CH), BF16),
            pltpu.VMEM((NZ, T, CH), BF16),
            pltpu.VMEM((NZ, 8, T), F32),
            pltpu.VMEM((T, CH), BF16),
            pltpu.VMEM((3, T, 2 * T), BF16),
            pltpu.VMEM((4, 8, T), F32),
            pltpu.VMEM((T, 2 * T), BF16),
            pltpu.VMEM((T, 2 * T), BF16),
            dma((6,)),
            dma((3, NP)),
            dma((3, NP)),
            dma((7,)),
            dma((NE,)),
            dma((2, 8)),
            dma((2, NE)),
            dma((2, 8)),
            dma((2, NE)),
            dma,
            dma,
            dma((7,)),
            dma((NE,)),
            dma((NP, 7)),
            dma((NP, NE)),
            dma((NP, 2)),
            dma((NZ,)),
            dma((NZ,)),
            dma((NZ,)),
            dma((3,)),
            dma((3,)),
            dma((3,)),
            dma((3,)),
        ],
        compiler_params=pltpu.CompilerParams(
            collective_id=0, has_side_effects=True, vmem_limit_bytes=59 * 1024 * 1024
        ),
        name="moe_layer",
    )(tokens, expert_ids.T, combine.T, cotangent, w_gate[0], w_up[0], w_down[0])
    mixed, gtok, gcomb, gg, gu, gd = settle(mixed, gtok, gcomb, gg, gu, gd)
    return mixed.T, gtok.T, gcomb.T, gg[None], gu[None], gd[None]


def solution(mesh):
    in_specs = (
        P("expert", None),
        P("expert", None),
        P("expert", None),
        P("expert", None),
        P("expert", None, "dp"),
        P("expert", None, "dp"),
        P("expert", "dp", None),
    )
    out_specs = (
        P("expert", "dp"),
        P("expert", "dp"),
        P("expert", None),
        P("expert", None, "dp"),
        P("expert", None, "dp"),
        P("expert", "dp", None),
    )
    return jax.shard_map(local, mesh=mesh, in_specs=in_specs, out_specs=out_specs, check_vma=False)
```

```python
import jax
import jax.numpy as jnp
from jax import lax
from jax.experimental import pallas as pl
from jax.experimental.pallas import tpu as pltpu
from jax.sharding import PartitionSpec as P

MESH = pl.DeviceIdType.MESH
F32 = jnp.float32
BF16 = jnp.bfloat16

T = 128
D = 3072
HD = 1536
QD = 768
CAP = 40
BLK = 2 * CAP
SLAB = 48
NE = 8
NZ = 8
W = 256
CH = 384
NP = 4

NS = 3

STEPS = ((0, 0), (2, 1), (2, 0), (0, 1), (1, 1), (3, 1), (1, 0), (3, 0))
HALVES = ((0, 1, 2, 3), (4, 5, 6, 7))
HR = 4 * CAP


def nn(a, b):
    return lax.dot_general(a, b, (((1,), (0,)), ((), ())), preferred_element_type=F32)


def nt(a, b):
    return lax.dot_general(a, b, (((1,), (1,)), ((), ())), preferred_element_type=F32)


def tn(a, b):
    return lax.dot_general(a, b, (((0,), (0,)), ((), ())), preferred_element_type=F32)


def iota(shape, axis):
    return lax.broadcasted_iota(jnp.int32, shape, axis)


def kernel(
    tok_hbm, ids_ref, comb_ref, cot_hbm, wg_hbm, wu_hbm, wd_hbm,
    mixed_ref, gtok_ref, gcomb_ref, og, ou, od,
    tc, wg, wu, wd, wgx, wux, wdx, slt, cwt, sendb, rows, acts, actx,
    gsend, grecv, tmat, psend, precv, rsend, rrecv, zsend, zrecv, gzrecv, ysend, yrecv, gycs,
    fsend, frecv,
    lsem, ws_s, ws_r, d_s, d_r, n_s, n_r, c_s, c_r, x_s, x_r, g_s, g_r, q_s, q_r, r_s, r_r,
    z_s, z_r, gz_s, gz_r, y_s, y_r, p_s, p_r,
):
    d = lax.axis_index("dp")
    e = lax.axis_index("expert")
    z, h, c = d // 4, (d // 2) % 2, d % 2
    yl, x = e // 4, e % 4
    twin = (z * 4 + h * 2 + (1 - c), e)
    over = (z * 4 + (1 - h) * 2 + c, e)

    goal = [((yl + dy) % 2) * 4 + (x + dx) % 4 for dx, dy in STEPS]
    origin = [((yl + dy) % 2) * 4 + (x + 4 - dx) % 4 for dx, dy in STEPS]

    def at_z(k):
        return (z + k) % NZ

    def zdev(zz):
        return (zz * 4 + h * 2 + c, e)

    def remote(src, dst, ssem, rsem, dev):
        return pltpu.make_async_remote_copy(
            src_ref=src, dst_ref=dst, send_sem=ssem, recv_sem=rsem, device_id=dev, device_id_type=MESH
        )

    par = z % 2
    quarter = pl.multiple_of(c * HD + par * QD, QD)
    mine = par == c
    last_to, last_from = at_z(5 + 2 * par), at_z(1 + 2 * par)
    last_to_over = (last_to * 4 + (1 - h) * 2 + c, e)
    last_from_over = (last_from * 4 + (1 - h) * 2 + c, e)
    near = (zdev(z + 1 - 2 * par), zdev((z + 2 * par + NZ - 1) % NZ))

    loads = [
        pltpu.make_async_copy(tok_hbm.at[:, pl.ds(quarter, QD)], tc.at[pl.ds(0, T)], lsem.at[0]),
        pltpu.make_async_copy(cot_hbm.at[:, pl.ds(quarter, QD)], tc.at[pl.ds(T, T)], lsem.at[1]),
        pltpu.make_async_copy(wg_hbm, wg, lsem.at[2]),
        pltpu.make_async_copy(wu_hbm, wu, lsem.at[3]),
        pltpu.make_async_copy(wd_hbm, wd, lsem.at[4]),
    ]
    for cp in loads:
        cp.start()

    barrier = pltpu.get_barrier_semaphore()
    for r in range(1, NE):
        pl.semaphore_signal(barrier, inc=1, device_id=(d, goal[r]), device_id_type=MESH)
    for k in range(1, NZ):
        pl.semaphore_signal(barrier, inc=1, device_id=zdev(at_z(k)), device_id_type=MESH)
    pl.semaphore_signal(barrier, inc=1, device_id=twin, device_id_type=MESH)
    pl.semaphore_signal(barrier, inc=1, device_id=over, device_id_type=MESH)
    pl.semaphore_signal(barrier, inc=1, device_id=last_to_over, device_id_type=MESH)
    pl.semaphore_signal(barrier, inc=1, device_id=last_from_over, device_id_type=MESH)

    deep = iota((T, T), 0)
    lane = iota((T, T), 1)
    ids = ids_ref[...]
    comb = comb_ref[...]
    pick0 = deep == ids[0:1]
    pick1 = deep == ids[1:2]
    chosen = jnp.logical_or(pick0, pick1)
    earlier = (deep < lane).astype(F32).astype(BF16)
    rank = nn(chosen.astype(F32).astype(BF16), earlier)
    slot = jnp.where(chosen, rank, -128.0)
    weight = jnp.where(pick0, comb[0:1], 0.0) + jnp.where(pick1, comb[1:2], 0.0)
    slt[...] = jnp.concatenate([slot[0:NE], slot[0:NE]], axis=1)
    cwt[...] = jnp.concatenate([jnp.ones((NE, T), F32), weight[0:NE]], axis=1)

    loads[0].wait()
    loads[1].wait()

    def pack(r):
        j = goal[r]
        slots = slt[pl.ds(j, 1), :]
        weights = cwt[pl.ds(j, 1), :]
        row = iota((BLK, 2 * T), 0)
        col = iota((BLK, 2 * T), 1)
        want = jnp.where(col < T, row, row - CAP).astype(F32)
        hit = want == slots
        scale = jnp.sum(jnp.where(hit, weights, 0.0), axis=1, keepdims=True)
        block = nn(hit.astype(F32).astype(BF16), tc[...])
        sendb[r] = (block * scale).astype(BF16)

    sends = []

    def go(cp):
        cp.start()
        sends.append(cp)

    def spread(r, src):
        for n in range(2):
            part = pl.ds(n * CH, CH)
            go(remote(src.at[:, part], rows.at[c, par, r, :, part], n_s.at[n, r], n_r.at[n, r], near[n]))
        go(remote(src, rows.at[c, par, r], c_s.at[0, r], c_r.at[0, r], twin))

    blocks_out = {r: remote(sendb.at[r], rows.at[c, par, r], d_s.at[r], d_r.at[r], (d, goal[r])) for r in range(1, NE)}
    for r in (1, 2, 3, 0, 4, 5, 6, 7):
        pack(r)
        if r == 1:
            pl.semaphore_wait(barrier, NE - 1 + NZ - 1 + 4)
        if r == 0:
            spread(0, sendb.at[0])
            own = pltpu.make_async_copy(sendb.at[0], rows.at[c, par, 0], lsem.at[5])
            own.start()
        elif r < 4:
            blocks_out[r].start()
    for r in (1, 2, 3):
        blocks_out[r].wait_send()
    for r in HALVES[1]:
        go(blocks_out[r])

    for m in range(NP):
        for n, (src, dst) in enumerate((
            (wd_hbm.at[:, pl.ds(pl.multiple_of((2 * m + 1 - c) * CH, CH), CH)], wdx.at[m]),
            (wg_hbm.at[pl.ds(pl.multiple_of((2 * m + c) * CH, CH), CH)], wgx.at[m]),
            (wu_hbm.at[pl.ds(pl.multiple_of((2 * m + c) * CH, CH), CH)], wux.at[m]),
        )):
            go(remote(src, dst, ws_s.at[n, m], ws_r.at[n, m], twin))

    def expert_of(at):
        return sum(jnp.where(at == r, goal[r], 0) for r in range(NE))

    column = iota((1, NE * BLK), 1)
    expand = (iota((T, NE * BLK), 0) == expert_of(column // BLK)).astype(F32).astype(BF16)
    weight_t = weight.T
    w_hi = weight_t.astype(BF16)
    w_lo = (weight_t - w_hi.astype(F32)).astype(BF16)
    inner = (column % BLK).astype(F32)
    slots_all = nn(slot.T.astype(BF16), expand)
    out_hit = slots_all == inner
    tmat[0:T] = jnp.where(out_hit, nn(w_hi, expand), 0.0).astype(BF16)
    tmat[T:2 * T] = jnp.where(out_hit, nn(w_lo, expand), 0.0).astype(BF16)
    tmat[2 * T:3 * T] = (slots_all == inner - CAP).astype(F32).astype(BF16)

    def pass_on(half):
        for r in HALVES[half]:
            if r:
                here = rows.at[c, par, r]
                remote(here, here, d_s.at[r], d_r.at[r], (d, goal[r])).wait_recv()
                spread(r, here)

    def pass_over(half):
        for r in HALVES[half]:
            there = rows.at[c, 1 - par, r]
            for n in range(2):
                part = there.at[:, pl.ds(n * CH, CH)]
                remote(part, part, n_s.at[n, r], n_r.at[n, r], near[n]).wait_recv()
            go(remote(there, there, c_s.at[1, r], c_r.at[1, r], twin))

    def from_twin(half, n):
        for r in HALVES[half]:
            there = rows.at[1 - c, (1 - par) if n else par, r]
            remote(there, there, c_s.at[n, r], c_r.at[n, r], twin).wait_recv()

    def x_rows(cc, pp, at=pl.ds(0, NE)):
        a = rows[cc, pp, at, 0:SLAB, :]
        return a.reshape(a.shape[0] * SLAB, QD)

    def e_rows(cc, pp, at=pl.ds(0, NE)):
        a = rows[cc, pp, at, BLK - SLAB:BLK, :]
        return a.reshape(a.shape[0] * SLAB, QD)

    def products(half, cc, pp, before=None):
        at = pl.ds(pl.multiple_of(cc * HD + pp * QD, QD), QD)
        blocks = pl.ds(half * 4, 4)
        xs = x_rows(cc, pp, blocks)
        new = nn(xs, wg[at, :]), nn(xs, wu[at, :]), nt(e_rows(cc, pp, blocks), wd[:, at])
        return new if before is None else tuple(u + v for u, v in zip(before, new))

    def first(a):
        return a.reshape(4, SLAB, W)[:, 0:CAP].reshape(HR, W)

    def last(a):
        return a.reshape(4, SLAB, W)[:, SLAB - CAP:].reshape(HR, W)

    swaps = []

    def activate(half, sum3):
        gate, up, hgrad = first(sum3[0]), first(sum3[1]), last(sum3[2])
        sig = jax.nn.sigmoid(gate)
        active = gate * sig
        hidden = (active * up).astype(BF16)
        mine_rows = pl.ds(half * HR, HR)
        acts[0, mine_rows] = hidden
        acts[1, mine_rows] = (hgrad * up * sig * (1.0 + gate * (1.0 - sig))).astype(BF16)
        acts[2, mine_rows] = (hgrad * active).astype(BF16)
        cp = remote(acts.at[:, mine_rows], actx.at[:, mine_rows], x_s.at[half], x_r.at[half], twin)
        go(cp)
        swaps.append(cp)
        dots = jnp.sum(hidden.astype(F32) * hgrad, axis=1, keepdims=True)
        gsend[half * 4:half * 4 + 4] = jnp.broadcast_to(dots, (HR, T)).reshape(4, CAP, T)
        for r in HALVES[half]:
            if r:
                go(remote(gsend.at[r], grecv.at[r], g_s.at[r], g_r.at[r], (d, origin[r])))
            else:
                grecv[0] = gsend[0]

    def by_parity(even, odd):
        return jnp.where(mine, even, odd), jnp.where(mine, odd, even)

    with_0 = at_z(6 - par)
    with_1 = at_z(2 + par)
    pairs_0 = ((with_0 + c) % NZ, (with_0 + 1 - c) % NZ)
    pairs_1 = ((with_1 + NZ - c) % NZ, (with_1 + NZ - 1 + c) % NZ)
    keep = jnp.where(par == 0, pairs_0[0], pairs_1[0]), jnp.where(par == 0, pairs_1[1], pairs_0[1])
    hand = jnp.where(par == 0, pairs_1[0], pairs_0[0]), jnp.where(par == 0, pairs_0[1], pairs_1[1])
    targets = (by_parity(at_z(4), at_z(3 - 2 * par)), keep, by_parity(z, last_to))

    def own_sums(half, to):
        at = pl.ds(half * HR, HR)
        oc = pl.multiple_of(to[0] * CH, CH)
        tcol = pl.multiple_of(to[1] * CH, CH)
        out = nn(acts[0, at], wd[:, pl.ds(oc, CH)])
        return out, nt(acts[1, at], wg[pl.ds(tcol, CH), :]) + nt(acts[2, at], wu[pl.ds(tcol, CH), :])

    def chip_sums(half, to, own_part=None):
        at = pl.ds(half * HR, HR)
        out, back = own_sums(half, to) if own_part is None else own_part
        out = out + nn(actx[0, at], wdx[to[0] // 2])
        return out, back + nt(actx[1, at], wgx[to[1] // 2]) + nt(actx[2, at], wux[to[1] // 2])

    def pair_copies(half):
        at = pl.ds(half * HR, HR)
        z_0, z_1 = z + 1 - 2 * par, (z + 2 * par + NZ - 1) % NZ
        to = zdev(jnp.where(par == 0, z_1, z_0)), zdev(jnp.where(par == 0, z_0, z_1))
        return [
            remote(psend.at[n, at], precv.at[n, at], q_s.at[half, n], q_r.at[half, n], to[n]) for n in range(2)
        ]

    def hand_over(half, own_part):
        at = pl.ds(half * HR, HR)
        sums = chip_sums(half, hand, own_part)
        for n in range(2):
            psend[n, at] = sums[n].astype(BF16)
        for cp in pair_copies(half):
            go(cp)

    given = []

    def give_back(half, s):
        out, back = chip_sums(half, targets[s])
        if s == 1:
            at = pl.ds(half * HR, HR)
            for cp in pair_copies(half):
                cp.wait_recv()
            out, back = out + precv[0, at].astype(F32), back + precv[1, at].astype(F32)
        both = jnp.concatenate([out.reshape(4, CAP, CH), back.reshape(4, CAP, CH)], axis=1)
        rsend[s, half * 4:half * 4 + 4] = both.astype(BF16)
        copies = [
            remote(rsend.at[s, r], rrecv.at[s, r], r_s.at[s, r], r_r.at[s, r], (d, origin[r]))
            for r in HALVES[half] if r
        ]
        if half == 0:
            rrecv[s, 0] = rsend[s, 0]
        if len(given) >= 2:
            for cp in given[-2]:
                cp.wait_send()
        for cp in copies:
            cp.start()
        given.append(copies)

    pass_on(0)
    own.wait()
    for cp in loads[2:]:
        cp.wait()
    sum_a = products(0, c, par)
    from_twin(0, 0)
    sum_a = products(0, 1 - c, par, sum_a)
    pass_on(1)
    sum_b = products(1, c, par)
    pass_over(0)
    sum_a = products(0, c, 1 - par, sum_a)
    from_twin(0, 1)
    sum_a = products(0, 1 - c, 1 - par, sum_a)
    activate(0, sum_a)
    from_twin(1, 0)
    sum_b = products(1, 1 - c, par, sum_b)
    start = own_sums(0, hand)
    for n in range(3):
        for m in range(NP):
            there = (wdx, wgx, wux)[n].at[m]
            remote(there, there, ws_s.at[n, m], ws_r.at[n, m], twin).wait_recv()
    swaps[0].wait_recv()
    hand_over(0, start)
    give_back(0, 0)
    give_back(0, 2)
    pass_over(1)
    sum_b = products(1, c, 1 - par, sum_b)
    from_twin(1, 1)
    sum_b = products(1, 1 - c, 1 - par, sum_b)
    activate(1, sum_b)
    start = own_sums(1, hand)
    swaps[1].wait_recv()
    hand_over(1, start)
    give_back(1, 0)
    give_back(0, 1)
    give_back(1, 1)

    for r in range(1, NE):
        remote(gsend.at[r], grecv.at[r], g_s.at[r], g_r.at[r], (d, goal[r])).wait_recv()
    q = iota((NE * CAP, T), 0).astype(F32)
    values = grecv[...].reshape(NE * CAP, T)

    slot_of = sum(jnp.where(deep == goal[r], r, 0) for r in range(1, NE)).astype(F32) * CAP + rank

    def gathered(pick, c_row):
        place = jnp.sum(jnp.where(pick, slot_of, 0.0), axis=0, keepdims=True)
        return jnp.sum(jnp.where(q == place, values, 0.0), axis=0, keepdims=True) / c_row

    sub = iota((8, T), 0)
    gzrecv[z] = jnp.where(
        sub == 0, gathered(pick0, comb[0:1]), jnp.where(sub == 1, gathered(pick1, comb[1:2]), 0.0)
    )
    for k in range(1, NZ):
        go(remote(gzrecv.at[z], gzrecv.at[z], gz_s.at[k], gz_r.at[z], zdev(at_z(k))))

    def padded(a, lead):
        a = a.astype(F32).reshape(NE, CAP, W)
        zero = jnp.zeros((NE, SLAB - CAP, W), F32)
        a = jnp.concatenate([a, zero] if lead else [zero, a], axis=1)
        return a.reshape(NE * SLAB, W).astype(BF16)

    hid_pad = padded(acts[0], False)
    pair_pad = jnp.concatenate([padded(acts[1], True), padded(acts[2], True)], axis=1)
    def weight_grads(k):
        at = k * QD
        both = tn(x_rows(k // 2, k % 2), pair_pad)
        og[at:at + QD] = both[:, 0:W].astype(BF16)
        ou[at:at + QD] = both[:, W:2 * W].astype(BF16)
        od[:, at:at + QD] = tn(hid_pad, e_rows(k // 2, k % 2)).astype(BF16)

    windows = [pl.ds(pl.multiple_of(T * hh, T), 2 * T) for hh in (h, 1 - h)]
    def to_tokens(s):
        for r in range(1, NE):
            remote(rsend.at[s, r], rrecv.at[s, r], r_s.at[s, r], r_r.at[s, r], (d, goal[r])).wait_recv()
        sums = nn(tmat[...], rrecv[s].reshape(NE * BLK, CH))
        mix = sums[0:T] + sums[T:2 * T]
        back = sums[2 * T:3 * T]
        if s < NS - 1:
            zsend[s, 0] = mix.astype(BF16)
            zsend[s, 1] = back.astype(BF16)
            for n in range(2):
                go(remote(zsend.at[s, n], zrecv.at[z], z_s.at[s, n], z_r.at[z], zdev(targets[s][n])))
        else:
            zsend[s, 0] = jnp.where(mine, back, mix).astype(BF16)
            for n, (src, dev) in enumerate((
                (zsend.at[s, 0, :, windows[0]], zdev(last_to)),
                (zsend.at[s, 0, :, windows[1]], last_to_over),
            )):
                go(remote(src, yrecv.at[n], y_s.at[n], y_r.at[n], dev))
            return jnp.where(mine, mix, back)

    give_back(1, 2)
    weight_grads(0)
    to_tokens(0)
    weight_grads(1)
    to_tokens(1)
    weight_grads(2)
    for k in range(1, NZ):
        zz = at_z(k)
        remote(gzrecv.at[zz], gzrecv.at[zz], gz_s.at[k], gz_r.at[zz], zdev(zz)).wait_recv()
    gc_sum = gzrecv[0]
    for k in range(1, NZ):
        gc_sum = gc_sum + gzrecv[k]
    gycs[0] = gc_sum
    gy = remote(gycs.at[0], gycs.at[1], p_s.at[0], p_r.at[0], over)
    gy.start()
    weight_grads(3)
    gy.wait_recv()
    gc_sum = gc_sum + gycs[1]
    gycs[2] = gc_sum
    gx = remote(gycs.at[2], gycs.at[3], p_s.at[1], p_r.at[1], twin)
    gx.start()
    total = to_tokens(NS - 1)
    steps = (
        4, jnp.where(par == 0, 1, 3),
        jnp.where(mine, 6 + par, 2 - par), jnp.where(mine, 3 - par, 5 + par),
    )
    for k in steps:
        zz = at_z(NZ - k)
        remote(zsend.at[0, 0], zrecv.at[zz], z_s.at[0, 0], z_r.at[zz], zdev(zz)).wait_recv()
        total = total + zrecv[zz].astype(F32)
    ysend[...] = total.astype(BF16)
    yc = remote(ysend.at[:, windows[1]], yrecv.at[2], y_s.at[2], y_r.at[2], over)
    yc.start()
    for n in range(3):
        remote(yrecv.at[n], yrecv.at[n], y_s.at[n], y_r.at[n], over).wait_recv()
    window = jnp.where(h == 0, total[:, 0:2 * T], total[:, T:3 * T])
    window = window + yrecv[0].astype(F32) + yrecv[1].astype(F32) + yrecv[2].astype(F32)
    final = window.astype(BF16)
    fsend[...] = final
    fc = remote(fsend, frecv, p_s.at[2], p_r.at[2], twin)
    fc.start()
    shift = 64 * h + 96 * c
    pick = (iota((T, 2 * T), 1) == iota((T, 2 * T), 0) + shift).astype(F32).astype(BF16)
    gx.wait_recv()
    gc_sum = gc_sum + gycs[3]
    gcomb_ref[...] = gc_sum[0:2]
    a = nt(pick, final)
    fc.wait_recv()
    b = nt(pick, frecv[...])
    mixed_ref[...] = jnp.where(mine, a, b)[0:96].astype(BF16)
    gtok_ref[...] = jnp.where(mine, b, a)[0:96].astype(BF16)

    for cp in sends + given[-2] + given[-1]:
        cp.wait_send()
    for cp in (gy, yc, gx, fc):
        cp.wait_send()


def settle_kernel(*refs):
    copies = [pltpu.make_async_copy(refs[i], refs[6 + i], refs[12].at[i]) for i in range(6)]
    for cp in copies:
        cp.start()
    for cp in copies:
        cp.wait()


def settle(*arrays):
    any_spec = pl.BlockSpec(memory_space=pl.ANY)
    return pl.pallas_call(
        settle_kernel,
        out_shape=tuple(jax.ShapeDtypeStruct(a.shape, a.dtype) for a in arrays),
        in_specs=[any_spec] * 6,
        out_specs=(any_spec,) * 6,
        scratch_shapes=[pltpu.SemaphoreType.DMA((6,))],
        compiler_params=pltpu.CompilerParams(vmem_limit_bytes=16 * 1024 * 1024),
        name="settle",
    )(*arrays)


def local(tokens, expert_ids, combine, cotangent, w_gate, w_up, w_down):
    any_spec = pl.BlockSpec(memory_space=pl.ANY)
    vmem = pl.BlockSpec(memory_space=pltpu.VMEM)
    dma = pltpu.SemaphoreType.DMA
    mixed, gtok, gcomb, gg, gu, gd = pl.pallas_call(
        kernel,
        out_shape=(
            pltpu.VMEM((96, T), BF16),
            pltpu.VMEM((96, T), BF16),
            pltpu.VMEM((2, T), F32),
            pltpu.VMEM((D, W), BF16),
            pltpu.VMEM((D, W), BF16),
            pltpu.VMEM((W, D), BF16),
        ),
        in_specs=[any_spec, vmem, vmem, any_spec, any_spec, any_spec, any_spec],
        out_specs=(vmem,) * 6,
        scratch_shapes=[
            pltpu.VMEM((2 * T, QD), BF16),
            pltpu.VMEM((D, W), BF16),
            pltpu.VMEM((D, W), BF16),
            pltpu.VMEM((W, D), BF16),
            pltpu.VMEM((NP, CH, W), BF16),
            pltpu.VMEM((NP, CH, W), BF16),
            pltpu.VMEM((NP, W, CH), BF16),
            pltpu.VMEM((NE, 2 * T), F32),
            pltpu.VMEM((NE, 2 * T), F32),
            pltpu.VMEM((NE, BLK, QD), BF16),
            pltpu.VMEM((2, 2, NE, BLK, QD), BF16),
            pltpu.VMEM((3, NE * CAP, W), BF16),
            pltpu.VMEM((3, NE * CAP, W), BF16),
            pltpu.VMEM((NE, CAP, T), F32),
            pltpu.VMEM((NE, CAP, T), F32),
            pltpu.VMEM((3 * T, NE * BLK), BF16),
            pltpu.VMEM((2, NE * CAP, CH), BF16),
            pltpu.VMEM((2, NE * CAP, CH), BF16),
            pltpu.VMEM((NS, NE, BLK, CH), BF16),
            pltpu.VMEM((NS, NE, BLK, CH), BF16),
            pltpu.VMEM((NS, 2, T, CH), BF16),
            pltpu.VMEM((NZ, T, CH), BF16),
            pltpu.VMEM((NZ, 8, T), F32),
            pltpu.VMEM((T, CH), BF16),
            pltpu.VMEM((3, T, 2 * T), BF16),
            pltpu.VMEM((4, 8, T), F32),
            pltpu.VMEM((T, 2 * T), BF16),
            pltpu.VMEM((T, 2 * T), BF16),
            dma((6,)),
            dma((3, NP)),
            dma((3, NP)),
            dma((NE,)),
            dma((NE,)),
            dma((2, 8)),
            dma((2, NE)),
            dma((2, 8)),
            dma((2, NE)),
            dma((2,)),
            dma((2,)),
            dma((NE,)),
            dma((NE,)),
            dma((2, 2)),
            dma((2, 2)),
            dma((NS, NE)),
            dma((NS, NE)),
            dma((NS, 2)),
            dma((NZ,)),
            dma((NZ,)),
            dma((NZ,)),
            dma((3,)),
            dma((3,)),
            dma((3,)),
            dma((3,)),
        ],
        compiler_params=pltpu.CompilerParams(
            collective_id=0, has_side_effects=True, vmem_limit_bytes=59 * 1024 * 1024
        ),
        name="moe_layer",
    )(tokens, expert_ids.T, combine.T, cotangent, w_gate[0], w_up[0], w_down[0])
    mixed, gtok, gcomb, gg, gu, gd = settle(mixed, gtok, gcomb, gg, gu, gd)
    return mixed.T, gtok.T, gcomb.T, gg[None], gu[None], gd[None]


def solution(mesh):
    in_specs = (
        P("expert", None),
        P("expert", None),
        P("expert", None),
        P("expert", None),
        P("expert", None, "dp"),
        P("expert", None, "dp"),
        P("expert", "dp", None),
    )
    out_specs = (
        P("expert", "dp"),
        P("expert", "dp"),
        P("expert", None),
        P("expert", None, "dp"),
        P("expert", None, "dp"),
        P("expert", "dp", None),
    )
    return jax.shard_map(local, mesh=mesh, in_specs=in_specs, out_specs=out_specs, check_vma=False)
```

```python
import jax
import jax.numpy as jnp
from jax import lax
from jax.experimental import pallas as pl
from jax.experimental.pallas import tpu as pltpu
from jax.sharding import PartitionSpec as P

MESH = pl.DeviceIdType.MESH
F32 = jnp.float32
BF16 = jnp.bfloat16

T = 128
D = 3072
HD = 1536
QD = 768
CAP = 40
BLK = 2 * CAP
SLAB = 48
NE = 8
NZ = 8
W = 256
CH = 384
NP = 4

NS = 3

STEPS = ((0, 0), (2, 1), (2, 0), (0, 1), (1, 1), (3, 1), (1, 0), (3, 0))
HALVES = ((0, 1, 2, 3), (4, 5, 6, 7))
WHOLE = (0, 6, 7)
HR = 4 * CAP


def nn(a, b):
    return lax.dot_general(a, b, (((1,), (0,)), ((), ())), preferred_element_type=F32)


def nt(a, b):
    return lax.dot_general(a, b, (((1,), (1,)), ((), ())), preferred_element_type=F32)


def tn(a, b):
    return lax.dot_general(a, b, (((0,), (0,)), ((), ())), preferred_element_type=F32)


def iota(shape, axis):
    return lax.broadcasted_iota(jnp.int32, shape, axis)


def kernel(
    tok_hbm, ids_ref, comb_ref, cot_hbm, wg_hbm, wu_hbm, wd_hbm,
    mixed_ref, gtok_ref, gcomb_ref, og, ou, od,
    tc, tc_2, wg, wu, wd, wgx, wux, wdx, slt, cwt, sendb, sendx, rows, acts, actx,
    gsend, grecv, tmat, psend, precv, rsend, rrecv, zsend, zrecv, gzrecv, ysend, yrecv, gycs,
    fsend, frecv,
    lsem, ws_s, ws_r, d_s, d_r, w_s, w_r, n_s, n_r, c_s, c_r, x_s, x_r, g_s, g_r, q_s, q_r, r_s, r_r,
    z_s, z_r, gz_s, gz_r, k_s, y_s, y_r, p_s, p_r,
):
    d = lax.axis_index("dp")
    e = lax.axis_index("expert")
    z, h, c = d // 4, (d // 2) % 2, d % 2
    yl, x = e // 4, e % 4
    twin = (z * 4 + h * 2 + (1 - c), e)
    over = (z * 4 + (1 - h) * 2 + c, e)

    goal = [((yl + dy) % 2) * 4 + (x + dx) % 4 for dx, dy in STEPS]
    origin = [((yl + dy) % 2) * 4 + (x + 4 - dx) % 4 for dx, dy in STEPS]

    def at_z(k):
        return (z + k) % NZ

    def zdev(zz):
        return (zz * 4 + h * 2 + c, e)

    def remote(src, dst, ssem, rsem, dev):
        return pltpu.make_async_remote_copy(
            src_ref=src, dst_ref=dst, send_sem=ssem, recv_sem=rsem, device_id=dev, device_id_type=MESH
        )

    par = z % 2
    quarter = pl.multiple_of(c * HD + par * QD, QD)
    quarter_2 = pl.multiple_of(c * HD + (1 - par) * QD, QD)
    mine = par == c
    up, down = 3 - 2 * par, 5 + 2 * par
    last_to = at_z(jnp.where(c == 0, down, up))
    last_from = at_z(jnp.where(c == 0, 1 + 2 * par, 7 - 2 * par))
    last_to_over = (last_to * 4 + (1 - h) * 2 + c, e)
    last_from_over = (last_from * 4 + (1 - h) * 2 + c, e)
    near = (zdev(z + 1 - 2 * par), zdev((z + 2 * par + NZ - 1) % NZ))

    loads = [
        pltpu.make_async_copy(tok_hbm.at[:, pl.ds(quarter, QD)], tc.at[pl.ds(0, T)], lsem.at[0]),
        pltpu.make_async_copy(cot_hbm.at[:, pl.ds(quarter, QD)], tc.at[pl.ds(T, T)], lsem.at[1]),
        pltpu.make_async_copy(tok_hbm.at[:, pl.ds(quarter_2, QD)], tc_2.at[pl.ds(0, T)], lsem.at[2]),
        pltpu.make_async_copy(cot_hbm.at[:, pl.ds(quarter_2, QD)], tc_2.at[pl.ds(T, T)], lsem.at[3]),
        pltpu.make_async_copy(wg_hbm, wg, lsem.at[4]),
        pltpu.make_async_copy(wu_hbm, wu, lsem.at[5]),
        pltpu.make_async_copy(wd_hbm, wd, lsem.at[6]),
    ]
    for cp in loads:
        cp.start()

    barrier = pltpu.get_barrier_semaphore()
    for r in range(1, NE):
        pl.semaphore_signal(barrier, inc=1, device_id=(d, goal[r]), device_id_type=MESH)
    for k in range(1, NZ):
        pl.semaphore_signal(barrier, inc=1, device_id=zdev(at_z(k)), device_id_type=MESH)
    pl.semaphore_signal(barrier, inc=1, device_id=twin, device_id_type=MESH)
    pl.semaphore_signal(barrier, inc=1, device_id=over, device_id_type=MESH)
    pl.semaphore_signal(barrier, inc=1, device_id=last_to_over, device_id_type=MESH)
    pl.semaphore_signal(barrier, inc=1, device_id=last_from_over, device_id_type=MESH)
    for k in (jnp.where(mine, 6 + par, 2 - par), jnp.where(mine, 3 - par, 5 + par)):
        giver = (at_z(NZ - k) * 4 + (1 - h) * 2 + c, e)
        pl.semaphore_signal(barrier, inc=1, device_id=giver, device_id_type=MESH)

    deep = iota((T, T), 0)
    lane = iota((T, T), 1)
    ids = ids_ref[...]
    comb = comb_ref[...]
    pick0 = deep == ids[0:1]
    pick1 = deep == ids[1:2]
    chosen = jnp.logical_or(pick0, pick1)
    earlier = (deep < lane).astype(F32).astype(BF16)
    rank = nn(chosen.astype(F32).astype(BF16), earlier)
    slot = jnp.where(chosen, rank, -128.0)
    weight = jnp.where(pick0, comb[0:1], 0.0) + jnp.where(pick1, comb[1:2], 0.0)
    slt[...] = jnp.concatenate([slot[0:NE], slot[0:NE]], axis=1)
    cwt[...] = jnp.concatenate([jnp.ones((NE, T), F32), weight[0:NE]], axis=1)

    loads[0].wait()
    loads[1].wait()

    def pack(r, source, to):
        j = goal[r]
        slots = slt[pl.ds(j, 1), :]
        weights = cwt[pl.ds(j, 1), :]
        row = iota((BLK, 2 * T), 0)
        col = iota((BLK, 2 * T), 1)
        want = jnp.where(col < T, row, row - CAP).astype(F32)
        hit = want == slots
        scale = jnp.sum(jnp.where(hit, weights, 0.0), axis=1, keepdims=True)
        block = nn(hit.astype(F32).astype(BF16), source[...])
        to[...] = (block * scale).astype(BF16)

    sends = []

    def go(cp):
        cp.start()
        sends.append(cp)

    def spread(r, src):
        for n in range(2 if r not in WHOLE else 0):
            part = pl.ds(n * CH, CH)
            go(remote(src.at[:, part], rows.at[c, par, r, :, part], n_s.at[n, r], n_r.at[n, r], near[n]))
        go(remote(src, rows.at[c, par, r], c_s.at[0, r], c_r.at[0, r], twin))

    blocks_out = {r: remote(sendb.at[r], rows.at[c, par, r], d_s.at[r], d_r.at[r], (d, goal[r])) for r in range(1, NE)}
    for r in (1, 2, 3, 0, 4, 5, 6, 7):
        pack(r, tc, sendb.at[r] if r else rows.at[c, par, 0])
        if r == 1:
            pl.semaphore_wait(barrier, NE - 1 + NZ - 1 + 6)
        if r == 0:
            spread(0, rows.at[c, par, 0])
        elif r < 4:
            blocks_out[r].start()
    for r in (1, 2, 3):
        blocks_out[r].wait_send()
    for r in HALVES[1]:
        blocks_out[r].start()
    loads[2].wait()
    loads[3].wait()
    for n, r in enumerate(WHOLE):
        pack(r, tc_2, sendx.at[n] if r else rows.at[c, 1 - par, 0])
    go(remote(rows.at[c, 1 - par, 0], rows.at[c, 1 - par, 0], c_s.at[1, 0], c_r.at[1, 0], twin))

    for m in range(NP):
        for n, (src, dst) in enumerate((
            (wd_hbm.at[:, pl.ds(pl.multiple_of((2 * m + 1 - c) * CH, CH), CH)], wdx.at[m]),
            (wg_hbm.at[pl.ds(pl.multiple_of((2 * m + c) * CH, CH), CH)], wgx.at[m]),
            (wu_hbm.at[pl.ds(pl.multiple_of((2 * m + c) * CH, CH), CH)], wux.at[m]),
        )):
            go(remote(src, dst, ws_s.at[n, m], ws_r.at[n, m], twin))

    def expert_of(at):
        return sum(jnp.where(at == r, goal[r], 0) for r in range(NE))

    column = iota((1, NE * BLK), 1)
    expand = (iota((T, NE * BLK), 0) == expert_of(column // BLK)).astype(F32).astype(BF16)
    weight_t = weight.T
    w_hi = weight_t.astype(BF16)
    w_lo = (weight_t - w_hi.astype(F32)).astype(BF16)
    inner = (column % BLK).astype(F32)
    slots_all = nn(slot.T.astype(BF16), expand)
    out_hit = slots_all == inner
    tmat[0:T] = jnp.where(out_hit, nn(w_hi, expand), 0.0).astype(BF16)
    tmat[T:2 * T] = jnp.where(out_hit, nn(w_lo, expand), 0.0).astype(BF16)
    tmat[2 * T:3 * T] = (slots_all == inner - CAP).astype(F32).astype(BF16)

    def pass_on(half):
        for r in HALVES[half]:
            if r:
                here = rows.at[c, par, r]
                remote(here, here, d_s.at[r], d_r.at[r], (d, goal[r])).wait_recv()
                spread(r, here)

    def pass_over(half):
        for r in HALVES[half]:
            if r == 0:
                continue
            there = rows.at[c, 1 - par, r]
            if r in WHOLE:
                remote(there, there, w_s.at[r], w_r.at[r], (d, goal[r])).wait_recv()
            for n in range(2 if r not in WHOLE else 0):
                part = there.at[:, pl.ds(n * CH, CH)]
                remote(part, part, n_s.at[n, r], n_r.at[n, r], near[n]).wait_recv()
            go(remote(there, there, c_s.at[1, r], c_r.at[1, r], twin))

    def from_twin(half, n):
        for r in HALVES[half]:
            there = rows.at[1 - c, (1 - par) if n else par, r]
            remote(there, there, c_s.at[n, r], c_r.at[n, r], twin).wait_recv()

    def x_rows(cc, pp, at=pl.ds(0, NE)):
        a = rows[cc, pp, at, 0:SLAB, :]
        return a.reshape(a.shape[0] * SLAB, QD)

    def e_rows(cc, pp, at=pl.ds(0, NE)):
        a = rows[cc, pp, at, BLK - SLAB:BLK, :]
        return a.reshape(a.shape[0] * SLAB, QD)

    def products(half, cc, pp, before=None):
        at = pl.ds(pl.multiple_of(cc * HD + pp * QD, QD), QD)
        blocks = pl.ds(half * 4, 4)
        xs = x_rows(cc, pp, blocks)
        new = nn(xs, wg[at, :]), nn(xs, wu[at, :]), nt(e_rows(cc, pp, blocks), wd[:, at])
        return new if before is None else tuple(u + v for u, v in zip(before, new))

    def first(a):
        return a.reshape(4, SLAB, W)[:, 0:CAP].reshape(HR, W)

    def last(a):
        return a.reshape(4, SLAB, W)[:, SLAB - CAP:].reshape(HR, W)

    swaps = []

    def activate(half, sum3):
        gate, up, hgrad = first(sum3[0]), first(sum3[1]), last(sum3[2])
        sig = jax.nn.sigmoid(gate)
        active = gate * sig
        hidden = (active * up).astype(BF16)
        mine_rows = pl.ds(half * HR, HR)
        acts[0, mine_rows] = hidden
        acts[1, mine_rows] = (hgrad * up * sig * (1.0 + gate * (1.0 - sig))).astype(BF16)
        acts[2, mine_rows] = (hgrad * active).astype(BF16)
        cp = remote(acts.at[:, mine_rows], actx.at[:, mine_rows], x_s.at[half], x_r.at[half], twin)
        go(cp)
        swaps.append(cp)
        dots = jnp.sum(hidden.astype(F32) * hgrad, axis=1, keepdims=True)
        gsend[half * 4:half * 4 + 4] = jnp.broadcast_to(dots, (HR, T)).reshape(4, CAP, T)
        for r in HALVES[half]:
            if r:
                go(remote(gsend.at[r], grecv.at[r], g_s.at[r], g_r.at[r], (d, origin[r])))
            else:
                grecv[0] = gsend[0]

    def by_parity(even, odd):
        return jnp.where(mine, even, odd), jnp.where(mine, odd, even)

    with_0 = at_z(6 - par)
    with_1 = at_z(2 + par)
    pairs_0 = ((with_0 + c) % NZ, (with_0 + 1 - c) % NZ)
    pairs_1 = ((with_1 + NZ - c) % NZ, (with_1 + NZ - 1 + c) % NZ)
    keep = jnp.where(par == 0, pairs_0[0], pairs_1[0]), jnp.where(par == 0, pairs_1[1], pairs_0[1])
    hand = jnp.where(par == 0, pairs_1[0], pairs_0[0]), jnp.where(par == 0, pairs_0[1], pairs_1[1])
    targets = (by_parity(at_z(4), at_z(jnp.where(c == 0, up, down))), keep, by_parity(z, last_to))

    def own_sums(half, to):
        at = pl.ds(half * HR, HR)
        oc = pl.multiple_of(to[0] * CH, CH)
        tcol = pl.multiple_of(to[1] * CH, CH)
        out = nn(acts[0, at], wd[:, pl.ds(oc, CH)])
        return out, nt(acts[1, at], wg[pl.ds(tcol, CH), :]) + nt(acts[2, at], wu[pl.ds(tcol, CH), :])

    def chip_sums(half, to, own_part=None):
        at = pl.ds(half * HR, HR)
        out, back = own_sums(half, to) if own_part is None else own_part
        out = out + nn(actx[0, at], wdx[to[0] // 2])
        return out, back + nt(actx[1, at], wgx[to[1] // 2]) + nt(actx[2, at], wux[to[1] // 2])

    def pair_copies(half):
        at = pl.ds(half * HR, HR)
        z_0, z_1 = z + 1 - 2 * par, (z + 2 * par + NZ - 1) % NZ
        to = zdev(jnp.where(par == 0, z_1, z_0)), zdev(jnp.where(par == 0, z_0, z_1))
        return [
            remote(psend.at[n, at], precv.at[n, at], q_s.at[half, n], q_r.at[half, n], to[n]) for n in range(2)
        ]

    def hand_over(half, own_part):
        at = pl.ds(half * HR, HR)
        sums = chip_sums(half, hand, own_part)
        for n in range(2):
            psend[n, at] = sums[n].astype(BF16)
        for cp in pair_copies(half):
            go(cp)

    def give_back(half, s):
        out, back = chip_sums(half, targets[s])
        if s == 1:
            at = pl.ds(half * HR, HR)
            for cp in pair_copies(half):
                cp.wait_recv()
            out, back = out + precv[0, at].astype(F32), back + precv[1, at].astype(F32)
        both = jnp.concatenate([out.reshape(4, CAP, CH), back.reshape(4, CAP, CH)], axis=1)
        rsend[s, half * 4:half * 4 + 4] = both.astype(BF16)
        copies = [
            remote(rsend.at[s, r], rrecv.at[s, r], r_s.at[s, r], r_r.at[s, r], (d, origin[r]))
            for r in HALVES[half] if r
        ]
        if half == 0:
            rrecv[s, 0] = rsend[s, 0]
        for cp in copies:
            go(cp)

    pass_on(0)
    for r in HALVES[1]:
        blocks_out[r].wait_send()
    for n, r in enumerate(WHOLE):
        if r:
            go(remote(sendx.at[n], rows.at[c, 1 - par, r], w_s.at[r], w_r.at[r], (d, goal[r])))
    for cp in loads[4:]:
        cp.wait()
    sum_a = products(0, c, par)
    from_twin(0, 0)
    sum_a = products(0, 1 - c, par, sum_a)
    pass_on(1)
    sum_b = products(1, c, par)
    pass_over(0)
    sum_a = products(0, c, 1 - par, sum_a)
    from_twin(0, 1)
    sum_a = products(0, 1 - c, 1 - par, sum_a)
    activate(0, sum_a)
    from_twin(1, 0)
    sum_b = products(1, 1 - c, par, sum_b)
    start = own_sums(0, hand)
    for n in range(3):
        for m in range(NP):
            there = (wdx, wgx, wux)[n].at[m]
            remote(there, there, ws_s.at[n, m], ws_r.at[n, m], twin).wait_recv()
    swaps[0].wait_recv()
    hand_over(0, start)
    give_back(0, 0)
    give_back(0, 2)
    pass_over(1)
    sum_b = products(1, c, 1 - par, sum_b)
    from_twin(1, 1)
    sum_b = products(1, 1 - c, 1 - par, sum_b)
    activate(1, sum_b)
    start = own_sums(1, hand)
    swaps[1].wait_recv()
    hand_over(1, start)
    give_back(1, 0)
    give_back(0, 1)
    give_back(1, 1)

    for r in range(1, NE):
        remote(gsend.at[r], grecv.at[r], g_s.at[r], g_r.at[r], (d, goal[r])).wait_recv()
    q = iota((NE * CAP, T), 0).astype(F32)
    values = grecv[...].reshape(NE * CAP, T)

    slot_of = sum(jnp.where(deep == goal[r], r, 0) for r in range(1, NE)).astype(F32) * CAP + rank

    def gathered(pick, c_row):
        place = jnp.sum(jnp.where(pick, slot_of, 0.0), axis=0, keepdims=True)
        return jnp.sum(jnp.where(q == place, values, 0.0), axis=0, keepdims=True) / c_row

    sub = iota((8, T), 0)
    gzrecv[z] = jnp.where(
        sub == 0, gathered(pick0, comb[0:1]), jnp.where(sub == 1, gathered(pick1, comb[1:2]), 0.0)
    )
    for k in range(1, NZ):
        go(remote(gzrecv.at[z], gzrecv.at[z], gz_s.at[k], gz_r.at[z], zdev(at_z(k))))

    def padded(a, lead):
        a = a.astype(F32).reshape(NE, CAP, W)
        zero = jnp.zeros((NE, SLAB - CAP, W), F32)
        a = jnp.concatenate([a, zero] if lead else [zero, a], axis=1)
        return a.reshape(NE * SLAB, W).astype(BF16)

    hid_pad = padded(acts[0], False)
    pair_pad = jnp.concatenate([padded(acts[1], True), padded(acts[2], True)], axis=1)
    def weight_grads(k):
        at = k * QD
        both = tn(x_rows(k // 2, k % 2), pair_pad)
        og[at:at + QD] = both[:, 0:W].astype(BF16)
        ou[at:at + QD] = both[:, W:2 * W].astype(BF16)
        od[:, at:at + QD] = tn(hid_pad, e_rows(k // 2, k % 2)).astype(BF16)

    windows = [pl.ds(pl.multiple_of(T * hh, T), 2 * T) for hh in (h, 1 - h)]
    def to_tokens(s):
        for r in range(1, NE):
            remote(rsend.at[s, r], rrecv.at[s, r], r_s.at[s, r], r_r.at[s, r], (d, goal[r])).wait_recv()
        sums = nn(tmat[...], rrecv[s].reshape(NE * BLK, CH))
        mix = sums[0:T] + sums[T:2 * T]
        back = sums[2 * T:3 * T]
        if s < NS - 1:
            zsend[s, 0] = mix.astype(BF16)
            zsend[s, 1] = back.astype(BF16)
            for n in range(2):
                if s == 1:
                    for w in range(2):
                        slot = 3 + 2 * par + w
                        dev = (targets[s][n] * 4 + (h + w) % 2 * 2 + c, e)
                        part = zsend.at[s, n, :, windows[w]]
                        go(remote(part, yrecv.at[slot], k_s.at[n, w], y_r.at[slot], dev))
                    continue
                go(remote(zsend.at[s, n], zrecv.at[z], z_s.at[s, n], z_r.at[z], zdev(targets[s][n])))
        else:
            zsend[s, 0] = jnp.where(mine, back, mix).astype(BF16)
            for n, (src, dev) in enumerate((
                (zsend.at[s, 0, :, windows[0]], zdev(last_to)),
                (zsend.at[s, 0, :, windows[1]], last_to_over),
            )):
                go(remote(src, yrecv.at[n], y_s.at[n], y_r.at[n], dev))
            return jnp.where(mine, mix, back)

    give_back(1, 2)
    weight_grads(0)
    to_tokens(0)
    weight_grads(1)
    to_tokens(1)
    weight_grads(2)
    weight_grads(3)
    total = to_tokens(NS - 1)
    for k in range(1, NZ):
        zz = at_z(k)
        remote(gzrecv.at[zz], gzrecv.at[zz], gz_s.at[k], gz_r.at[zz], zdev(zz)).wait_recv()
    gc_sum = gzrecv[0]
    for k in range(1, NZ):
        gc_sum = gc_sum + gzrecv[k]
    gycs[0] = gc_sum
    gy = remote(gycs.at[0], gycs.at[1], p_s.at[0], p_r.at[0], over)
    gy.start()
    for k in (4, jnp.where(c == 0, 1 + 2 * par, 7 - 2 * par)):
        zz = at_z(NZ - k)
        remote(zsend.at[0, 0], zrecv.at[zz], z_s.at[0, 0], z_r.at[zz], zdev(zz)).wait_recv()
        total = total + zrecv[zz].astype(F32)
    ysend[...] = total.astype(BF16)
    yc = remote(ysend.at[:, windows[1]], yrecv.at[2], y_s.at[2], y_r.at[2], over)
    yc.start()
    gy.wait_recv()
    gc_sum = gc_sum + gycs[1]
    gycs[2] = gc_sum
    gx = remote(gycs.at[2], gycs.at[3], p_s.at[1], p_r.at[1], twin)
    gx.start()
    for n in range(7):
        remote(yrecv.at[n], yrecv.at[n], y_s.at[0], y_r.at[n], over).wait_recv()
    window = jnp.where(h == 0, total[:, 0:2 * T], total[:, T:3 * T])
    for n in range(7):
        window = window + yrecv[n].astype(F32)
    final = window.astype(BF16)
    fsend[...] = final
    fc = remote(fsend, frecv, p_s.at[2], p_r.at[2], twin)
    fc.start()
    shift = 64 * h + 96 * c
    pick = (iota((T, 2 * T), 1) == iota((T, 2 * T), 0) + shift).astype(F32).astype(BF16)
    gx.wait_recv()
    gc_sum = gc_sum + gycs[3]
    gcomb_ref[...] = gc_sum[0:2]
    a = nt(pick, final)
    fc.wait_recv()
    b = nt(pick, frecv[...])
    mixed_ref[...] = jnp.where(mine, a, b)[0:96].astype(BF16)
    gtok_ref[...] = jnp.where(mine, b, a)[0:96].astype(BF16)

    for cp in sends:
        cp.wait_send()
    for cp in (gy, yc, gx, fc):
        cp.wait_send()


def settle_kernel(*refs):
    copies = [pltpu.make_async_copy(refs[i], refs[6 + i], refs[12].at[i]) for i in range(6)]
    for cp in copies:
        cp.start()
    for cp in copies:
        cp.wait()


def settle(*arrays):
    any_spec = pl.BlockSpec(memory_space=pl.ANY)
    return pl.pallas_call(
        settle_kernel,
        out_shape=tuple(jax.ShapeDtypeStruct(a.shape, a.dtype) for a in arrays),
        in_specs=[any_spec] * 6,
        out_specs=(any_spec,) * 6,
        scratch_shapes=[pltpu.SemaphoreType.DMA((6,))],
        compiler_params=pltpu.CompilerParams(vmem_limit_bytes=16 * 1024 * 1024),
        name="settle",
    )(*arrays)


def local(tokens, expert_ids, combine, cotangent, w_gate, w_up, w_down):
    any_spec = pl.BlockSpec(memory_space=pl.ANY)
    vmem = pl.BlockSpec(memory_space=pltpu.VMEM)
    dma = pltpu.SemaphoreType.DMA
    mixed, gtok, gcomb, gg, gu, gd = pl.pallas_call(
        kernel,
        out_shape=(
            pltpu.VMEM((96, T), BF16),
            pltpu.VMEM((96, T), BF16),
            pltpu.VMEM((2, T), F32),
            pltpu.VMEM((D, W), BF16),
            pltpu.VMEM((D, W), BF16),
            pltpu.VMEM((W, D), BF16),
        ),
        in_specs=[any_spec, vmem, vmem, any_spec, any_spec, any_spec, any_spec],
        out_specs=(vmem,) * 6,
        scratch_shapes=[
            pltpu.VMEM((2 * T, QD), BF16),
            pltpu.VMEM((2 * T, QD), BF16),
            pltpu.VMEM((D, W), BF16),
            pltpu.VMEM((D, W), BF16),
            pltpu.VMEM((W, D), BF16),
            pltpu.VMEM((NP, CH, W), BF16),
            pltpu.VMEM((NP, CH, W), BF16),
            pltpu.VMEM((NP, W, CH), BF16),
            pltpu.VMEM((NE, 2 * T), F32),
            pltpu.VMEM((NE, 2 * T), F32),
            pltpu.VMEM((NE, BLK, QD), BF16),
            pltpu.VMEM((3, BLK, QD), BF16),
            pltpu.VMEM((2, 2, NE, BLK, QD), BF16),
            pltpu.VMEM((3, NE * CAP, W), BF16),
            pltpu.VMEM((3, NE * CAP, W), BF16),
            pltpu.VMEM((NE, CAP, T), F32),
            pltpu.VMEM((NE, CAP, T), F32),
            pltpu.VMEM((3 * T, NE * BLK), BF16),
            pltpu.VMEM((2, NE * CAP, CH), BF16),
            pltpu.VMEM((2, NE * CAP, CH), BF16),
            pltpu.VMEM((NS, NE, BLK, CH), BF16),
            pltpu.VMEM((NS, NE, BLK, CH), BF16),
            pltpu.VMEM((NS, 2, T, CH), BF16),
            pltpu.VMEM((NZ, T, CH), BF16),
            pltpu.VMEM((NZ, 8, T), F32),
            pltpu.VMEM((T, CH), BF16),
            pltpu.VMEM((7, T, 2 * T), BF16),
            pltpu.VMEM((4, 8, T), F32),
            pltpu.VMEM((T, 2 * T), BF16),
            pltpu.VMEM((T, 2 * T), BF16),
            dma((7,)),
            dma((3, NP)),
            dma((3, NP)),
            dma((NE,)),
            dma((NE,)),
            dma((NE,)),
            dma((NE,)),
            dma((2, 8)),
            dma((2, NE)),
            dma((2, 8)),
            dma((2, NE)),
            dma((2,)),
            dma((2,)),
            dma((NE,)),
            dma((NE,)),
            dma((2, 2)),
            dma((2, 2)),
            dma((NS, NE)),
            dma((NS, NE)),
            dma((NS, 2)),
            dma((NZ,)),
            dma((NZ,)),
            dma((NZ,)),
            dma((2, 2)),
            dma((3,)),
            dma((7,)),
            dma((3,)),
            dma((3,)),
        ],
        compiler_params=pltpu.CompilerParams(
            collective_id=0, has_side_effects=True, vmem_limit_bytes=59 * 1024 * 1024
        ),
        name="moe_layer",
    )(tokens, expert_ids.T, combine.T, cotangent, w_gate[0], w_up[0], w_down[0])
    mixed, gtok, gcomb, gg, gu, gd = settle(mixed, gtok, gcomb, gg, gu, gd)
    return mixed.T, gtok.T, gcomb.T, gg[None], gu[None], gd[None]


def solution(mesh):
    in_specs = (
        P("expert", None),
        P("expert", None),
        P("expert", None),
        P("expert", None),
        P("expert", None, "dp"),
        P("expert", None, "dp"),
        P("expert", "dp", None),
    )
    out_specs = (
        P("expert", "dp"),
        P("expert", "dp"),
        P("expert", None),
        P("expert", None, "dp"),
        P("expert", None, "dp"),
        P("expert", "dp", None),
    )
    return jax.shard_map(local, mesh=mesh, in_specs=in_specs, out_specs=out_specs, check_vma=False)
```

```python
import jax
import jax.numpy as jnp
from jax import lax
from jax.experimental import pallas as pl
from jax.experimental.pallas import tpu as pltpu
from jax.sharding import PartitionSpec as P

MESH = pl.DeviceIdType.MESH
F32 = jnp.float32
BF16 = jnp.bfloat16

T = 128
D = 3072
HD = 1536
QD = 768
CAP = 40
BLK = 2 * CAP
SLAB = 48
NE = 8
NZ = 8
W = 256
CH = 384
NP = 4

NS = 3

STEPS = ((0, 0), (2, 1), (2, 0), (0, 1), (1, 1), (3, 1), (1, 0), (3, 0))
HALVES = ((0, 1, 2, 3), (4, 5, 6, 7))
WHOLE = (0, 6, 7)
HR = 4 * CAP


def nn(a, b):
    return lax.dot_general(a, b, (((1,), (0,)), ((), ())), preferred_element_type=F32)


def nt(a, b):
    return lax.dot_general(a, b, (((1,), (1,)), ((), ())), preferred_element_type=F32)


def tn(a, b):
    return lax.dot_general(a, b, (((0,), (0,)), ((), ())), preferred_element_type=F32)


def iota(shape, axis):
    return lax.broadcasted_iota(jnp.int32, shape, axis)


def kernel(
    tok_hbm, ids_ref, comb_ref, cot_hbm, wg_hbm, wu_hbm, wd_hbm,
    mixed_ref, gtok_ref, gcomb_ref, og, ou, od,
    tc, tc_2, wg, wu, wd, wgx, wux, wdx, slt, cwt, sendb, sendx, rows, acts, actx,
    gsend, grecv, tmat, psend, precv, rsend, rrecv, zsend, zrecv, gzrecv, ysend, yrecv, gycs,
    fsend, frecv,
    lsem, ws_s, ws_r, d_s, d_r, w_s, w_r, n_s, n_r, c_s, c_r, x_s, x_r, g_s, g_r, q_s, q_r, r_s, r_r,
    z_s, z_r, gz_s, gz_r, k_s, y_s, y_r, p_s, p_r,
):
    d = lax.axis_index("dp")
    e = lax.axis_index("expert")
    z, h, c = d // 4, (d // 2) % 2, d % 2
    yl, x = e // 4, e % 4
    twin = (z * 4 + h * 2 + (1 - c), e)
    over = (z * 4 + (1 - h) * 2 + c, e)

    goal = [((yl + dy) % 2) * 4 + (x + dx) % 4 for dx, dy in STEPS]
    origin = [((yl + dy) % 2) * 4 + (x + 4 - dx) % 4 for dx, dy in STEPS]

    def at_z(k):
        return (z + k) % NZ

    def zdev(zz):
        return (zz * 4 + h * 2 + c, e)

    def remote(src, dst, ssem, rsem, dev):
        return pltpu.make_async_remote_copy(
            src_ref=src, dst_ref=dst, send_sem=ssem, recv_sem=rsem, device_id=dev, device_id_type=MESH
        )

    par = z % 2
    quarter = pl.multiple_of(c * HD + par * QD, QD)
    quarter_2 = pl.multiple_of(c * HD + (1 - par) * QD, QD)
    mine = par == c
    up, down = 1, NZ - 1
    last_to = at_z(jnp.where(c == 0, down, up))
    last_from = at_z(jnp.where(c == 0, up, down))
    last_to_over = (last_to * 4 + (1 - h) * 2 + c, e)
    last_from_over = (last_from * 4 + (1 - h) * 2 + c, e)
    near = (zdev(z + 1 - 2 * par), zdev((z + 2 * par + NZ - 1) % NZ))

    barrier = pltpu.get_barrier_semaphore()
    for r in range(1, NE):
        pl.semaphore_signal(barrier, inc=1, device_id=(d, goal[r]), device_id_type=MESH)
    for k in range(1, NZ):
        pl.semaphore_signal(barrier, inc=1, device_id=zdev(at_z(k)), device_id_type=MESH)
    pl.semaphore_signal(barrier, inc=1, device_id=twin, device_id_type=MESH)
    pl.semaphore_signal(barrier, inc=1, device_id=over, device_id_type=MESH)
    pl.semaphore_signal(barrier, inc=1, device_id=last_to_over, device_id_type=MESH)
    pl.semaphore_signal(barrier, inc=1, device_id=last_from_over, device_id_type=MESH)
    for k in (jnp.where(mine, 6, 2), jnp.where(mine, 3, 5)):
        giver = (at_z(NZ - k) * 4 + (1 - h) * 2 + c, e)
        pl.semaphore_signal(barrier, inc=1, device_id=giver, device_id_type=MESH)

    loads = [
        pltpu.make_async_copy(tok_hbm.at[:, pl.ds(quarter, QD)], tc.at[pl.ds(0, T)], lsem.at[0]),
        pltpu.make_async_copy(cot_hbm.at[:, pl.ds(quarter, QD)], tc.at[pl.ds(T, T)], lsem.at[1]),
        pltpu.make_async_copy(tok_hbm.at[:, pl.ds(quarter_2, QD)], tc_2.at[pl.ds(0, T)], lsem.at[2]),
        pltpu.make_async_copy(cot_hbm.at[:, pl.ds(quarter_2, QD)], tc_2.at[pl.ds(T, T)], lsem.at[3]),
        pltpu.make_async_copy(wg_hbm, wg, lsem.at[4]),
        pltpu.make_async_copy(wu_hbm, wu, lsem.at[5]),
        pltpu.make_async_copy(wd_hbm, wd, lsem.at[6]),
    ]
    for cp in loads:
        cp.start()

    deep = iota((T, T), 0)
    lane = iota((T, T), 1)
    ids = ids_ref[...]
    comb = comb_ref[...]
    pick0 = deep == ids[0:1]
    pick1 = deep == ids[1:2]
    chosen = jnp.logical_or(pick0, pick1)
    earlier = (deep < lane).astype(F32).astype(BF16)
    rank = nn(chosen.astype(F32).astype(BF16), earlier)
    slot = jnp.where(chosen, rank, -128.0)
    weight = jnp.where(pick0, comb[0:1], 0.0) + jnp.where(pick1, comb[1:2], 0.0)
    slt[...] = jnp.concatenate([slot[0:NE], slot[0:NE]], axis=1)
    cwt[...] = jnp.concatenate([jnp.ones((NE, T), F32), weight[0:NE]], axis=1)

    loads[0].wait()
    loads[1].wait()

    def pack(r, source, to):
        j = goal[r]
        slots = slt[pl.ds(j, 1), :]
        weights = cwt[pl.ds(j, 1), :]
        row = iota((BLK, 2 * T), 0)
        col = iota((BLK, 2 * T), 1)
        want = jnp.where(col < T, row, row - CAP).astype(F32)
        hit = want == slots
        scale = jnp.sum(jnp.where(hit, weights, 0.0), axis=1, keepdims=True)
        block = nn(hit.astype(F32).astype(BF16), source[...])
        to[...] = (block * scale).astype(BF16)

    sends = []

    def go(cp):
        cp.start()
        sends.append(cp)

    def spread(r, src):
        for n in range(2 if r not in WHOLE else 0):
            part = pl.ds(n * CH, CH)
            go(remote(src.at[:, part], rows.at[c, par, r, :, part], n_s.at[n, r], n_r.at[n, r], near[n]))
        go(remote(src, rows.at[c, par, r], c_s.at[0, r], c_r.at[0, r], twin))

    blocks_out = {r: remote(sendb.at[r], rows.at[c, par, r], d_s.at[r], d_r.at[r], (d, goal[r])) for r in range(1, NE)}
    for r in (1, 2, 3, 0, 4, 5, 6, 7):
        pack(r, tc, sendb.at[r] if r else rows.at[c, par, 0])
        if r == 1:
            pl.semaphore_wait(barrier, NE - 1 + NZ - 1 + 6)
        if r == 0:
            spread(0, rows.at[c, par, 0])
        elif r < 4:
            blocks_out[r].start()
    for r in (1, 2, 3):
        blocks_out[r].wait_send()
    for r in HALVES[1]:
        blocks_out[r].start()
    loads[2].wait()
    loads[3].wait()
    for n, r in enumerate(WHOLE):
        pack(r, tc_2, sendx.at[n] if r else rows.at[c, 1 - par, 0])
    go(remote(rows.at[c, 1 - par, 0], rows.at[c, 1 - par, 0], c_s.at[1, 0], c_r.at[1, 0], twin))

    for m in range(NP):
        for n, (src, dst) in enumerate((
            (wd_hbm.at[:, pl.ds(pl.multiple_of((2 * m + 1 - c) * CH, CH), CH)], wdx.at[m]),
            (wg_hbm.at[pl.ds(pl.multiple_of((2 * m + c) * CH, CH), CH)], wgx.at[m]),
            (wu_hbm.at[pl.ds(pl.multiple_of((2 * m + c) * CH, CH), CH)], wux.at[m]),
        )):
            go(remote(src, dst, ws_s.at[n, m], ws_r.at[n, m], twin))

    def expert_of(at):
        return sum(jnp.where(at == r, goal[r], 0) for r in range(NE))

    column = iota((1, NE * BLK), 1)
    expand = (iota((T, NE * BLK), 0) == expert_of(column // BLK)).astype(F32).astype(BF16)
    weight_t = weight.T
    w_hi = weight_t.astype(BF16)
    w_lo = (weight_t - w_hi.astype(F32)).astype(BF16)
    inner = (column % BLK).astype(F32)
    slots_all = nn(slot.T.astype(BF16), expand)
    out_hit = slots_all == inner
    tmat[0:T] = jnp.where(out_hit, nn(w_hi, expand), 0.0).astype(BF16)
    tmat[T:2 * T] = jnp.where(out_hit, nn(w_lo, expand), 0.0).astype(BF16)
    tmat[2 * T:3 * T] = (slots_all == inner - CAP).astype(F32).astype(BF16)

    def pass_on(half):
        for r in HALVES[half]:
            if r:
                here = rows.at[c, par, r]
                remote(here, here, d_s.at[r], d_r.at[r], (d, goal[r])).wait_recv()
                spread(r, here)

    def pass_over(half):
        for r in HALVES[half]:
            if r == 0:
                continue
            there = rows.at[c, 1 - par, r]
            if r in WHOLE:
                remote(there, there, w_s.at[r], w_r.at[r], (d, goal[r])).wait_recv()
            for n in range(2 if r not in WHOLE else 0):
                part = there.at[:, pl.ds(n * CH, CH)]
                remote(part, part, n_s.at[n, r], n_r.at[n, r], near[n]).wait_recv()
            go(remote(there, there, c_s.at[1, r], c_r.at[1, r], twin))

    def from_twin(half, n):
        for r in HALVES[half]:
            there = rows.at[1 - c, (1 - par) if n else par, r]
            remote(there, there, c_s.at[n, r], c_r.at[n, r], twin).wait_recv()

    def x_rows(cc, pp, at=pl.ds(0, NE)):
        a = rows[cc, pp, at, 0:SLAB, :]
        return a.reshape(a.shape[0] * SLAB, QD)

    def e_rows(cc, pp, at=pl.ds(0, NE)):
        a = rows[cc, pp, at, BLK - SLAB:BLK, :]
        return a.reshape(a.shape[0] * SLAB, QD)

    def products(half, cc, pp, before=None):
        at = pl.ds(pl.multiple_of(cc * HD + pp * QD, QD), QD)
        blocks = pl.ds(half * 4, 4)
        xs = x_rows(cc, pp, blocks)
        new = nn(xs, wg[at, :]), nn(xs, wu[at, :]), nt(e_rows(cc, pp, blocks), wd[:, at])
        return new if before is None else tuple(u + v for u, v in zip(before, new))

    def first(a):
        return a.reshape(4, SLAB, W)[:, 0:CAP].reshape(HR, W)

    def last(a):
        return a.reshape(4, SLAB, W)[:, SLAB - CAP:].reshape(HR, W)

    swaps = []

    def activate(half, sum3):
        gate, up, hgrad = first(sum3[0]), first(sum3[1]), last(sum3[2])
        sig = jax.nn.sigmoid(gate)
        active = gate * sig
        hidden = (active * up).astype(BF16)
        mine_rows = pl.ds(half * HR, HR)
        acts[0, mine_rows] = hidden
        acts[1, mine_rows] = (hgrad * up * sig * (1.0 + gate * (1.0 - sig))).astype(BF16)
        acts[2, mine_rows] = (hgrad * active).astype(BF16)
        cp = remote(acts.at[:, mine_rows], actx.at[:, mine_rows], x_s.at[half], x_r.at[half], twin)
        go(cp)
        swaps.append(cp)
        dots = jnp.sum(hidden.astype(F32) * hgrad, axis=1, keepdims=True)
        gsend[half * 4:half * 4 + 4] = jnp.broadcast_to(dots, (HR, T)).reshape(4, CAP, T)
        for r in HALVES[half]:
            if r:
                go(remote(gsend.at[r], grecv.at[r], g_s.at[r], g_r.at[r], (d, origin[r])))
            else:
                grecv[0] = gsend[0]

    def by_parity(even, odd):
        return jnp.where(mine, even, odd), jnp.where(mine, odd, even)

    with_0 = at_z(6 - par), at_z(3 - par)
    with_1 = at_z(2 + par), at_z(5 + par)
    pairs_0 = [jnp.where(c == n, with_0[0], with_0[1]) for n in range(2)]
    pairs_1 = [jnp.where(c == n, with_1[0], with_1[1]) for n in range(2)]
    keep = jnp.where(par == 0, pairs_0[0], pairs_1[0]), jnp.where(par == 0, pairs_1[1], pairs_0[1])
    hand = jnp.where(par == 0, pairs_1[0], pairs_0[0]), jnp.where(par == 0, pairs_0[1], pairs_1[1])
    targets = (by_parity(at_z(4), at_z(jnp.where(c == 0, up, down))), keep, by_parity(z, last_to))

    def own_sums(half, to):
        at = pl.ds(half * HR, HR)
        oc = pl.multiple_of(to[0] * CH, CH)
        tcol = pl.multiple_of(to[1] * CH, CH)
        out = nn(acts[0, at], wd[:, pl.ds(oc, CH)])
        return out, nt(acts[1, at], wg[pl.ds(tcol, CH), :]) + nt(acts[2, at], wu[pl.ds(tcol, CH), :])

    def chip_sums(half, to, own_part=None):
        at = pl.ds(half * HR, HR)
        out, back = own_sums(half, to) if own_part is None else own_part
        out = out + nn(actx[0, at], wdx[to[0] // 2])
        return out, back + nt(actx[1, at], wgx[to[1] // 2]) + nt(actx[2, at], wux[to[1] // 2])

    def pair_copies(half):
        at = pl.ds(half * HR, HR)
        z_0, z_1 = z + 1 - 2 * par, (z + 2 * par + NZ - 1) % NZ
        to = zdev(jnp.where(par == 0, z_1, z_0)), zdev(jnp.where(par == 0, z_0, z_1))
        return [
            remote(psend.at[n, at], precv.at[n, at], q_s.at[half, n], q_r.at[half, n], to[n]) for n in range(2)
        ]

    def hand_over(half, own_part):
        at = pl.ds(half * HR, HR)
        sums = chip_sums(half, hand, own_part)
        for n in range(2):
            psend[n, at] = sums[n].astype(BF16)
        for cp in pair_copies(half):
            go(cp)

    def give_back(half, s):
        out, back = chip_sums(half, targets[s])
        if s == 1:
            at = pl.ds(half * HR, HR)
            for cp in pair_copies(half):
                cp.wait_recv()
            out, back = out + precv[0, at].astype(F32), back + precv[1, at].astype(F32)
        both = jnp.concatenate([out.reshape(4, CAP, CH), back.reshape(4, CAP, CH)], axis=1)
        rsend[s, half * 4:half * 4 + 4] = both.astype(BF16)
        copies = [
            remote(rsend.at[s, r], rrecv.at[s, r], r_s.at[s, r], r_r.at[s, r], (d, origin[r]))
            for r in HALVES[half] if r
        ]
        if half == 0:
            rrecv[s, 0] = rsend[s, 0]
        for cp in copies:
            go(cp)

    pass_on(0)
    for r in HALVES[1]:
        blocks_out[r].wait_send()
    for n, r in enumerate(WHOLE):
        if r:
            go(remote(sendx.at[n], rows.at[c, 1 - par, r], w_s.at[r], w_r.at[r], (d, goal[r])))
    for cp in loads[4:]:
        cp.wait()
    sum_a = products(0, c, par)
    from_twin(0, 0)
    sum_a = products(0, 1 - c, par, sum_a)
    pass_on(1)
    sum_b = products(1, c, par)
    pass_over(0)
    sum_a = products(0, c, 1 - par, sum_a)
    from_twin(0, 1)
    sum_a = products(0, 1 - c, 1 - par, sum_a)
    activate(0, sum_a)
    from_twin(1, 0)
    sum_b = products(1, 1 - c, par, sum_b)
    start = own_sums(0, hand)
    for n in range(3):
        for m in range(NP):
            there = (wdx, wgx, wux)[n].at[m]
            remote(there, there, ws_s.at[n, m], ws_r.at[n, m], twin).wait_recv()
    swaps[0].wait_recv()
    hand_over(0, start)
    give_back(0, 0)
    give_back(0, 2)
    pass_over(1)
    sum_b = products(1, c, 1 - par, sum_b)
    from_twin(1, 1)
    sum_b = products(1, 1 - c, 1 - par, sum_b)
    activate(1, sum_b)
    start = own_sums(1, hand)
    swaps[1].wait_recv()
    hand_over(1, start)
    give_back(1, 0)
    give_back(0, 1)
    give_back(1, 1)

    for r in range(1, NE):
        remote(gsend.at[r], grecv.at[r], g_s.at[r], g_r.at[r], (d, goal[r])).wait_recv()
    q = iota((NE * CAP, T), 0).astype(F32)
    values = grecv[...].reshape(NE * CAP, T)

    slot_of = sum(jnp.where(deep == goal[r], r, 0) for r in range(1, NE)).astype(F32) * CAP + rank

    def gathered(pick, c_row):
        place = jnp.sum(jnp.where(pick, slot_of, 0.0), axis=0, keepdims=True)
        return jnp.sum(jnp.where(q == place, values, 0.0), axis=0, keepdims=True) / c_row

    sub = iota((8, T), 0)
    gzrecv[z] = jnp.where(
        sub == 0, gathered(pick0, comb[0:1]), jnp.where(sub == 1, gathered(pick1, comb[1:2]), 0.0)
    )
    for k in range(1, NZ):
        go(remote(gzrecv.at[z], gzrecv.at[z], gz_s.at[k], gz_r.at[z], zdev(at_z(k))))

    def padded(a, lead):
        a = a.astype(F32).reshape(NE, CAP, W)
        zero = jnp.zeros((NE, SLAB - CAP, W), F32)
        a = jnp.concatenate([a, zero] if lead else [zero, a], axis=1)
        return a.reshape(NE * SLAB, W).astype(BF16)

    hid_pad = padded(acts[0], False)
    pair_pad = jnp.concatenate([padded(acts[1], True), padded(acts[2], True)], axis=1)
    def weight_grads(k):
        at = k * QD
        both = tn(x_rows(k // 2, k % 2), pair_pad)
        og[at:at + QD] = both[:, 0:W].astype(BF16)
        ou[at:at + QD] = both[:, W:2 * W].astype(BF16)
        od[:, at:at + QD] = tn(hid_pad, e_rows(k // 2, k % 2)).astype(BF16)

    windows = [pl.ds(pl.multiple_of(T * hh, T), 2 * T) for hh in (h, 1 - h)]
    def to_tokens(s):
        for r in range(1, NE):
            remote(rsend.at[s, r], rrecv.at[s, r], r_s.at[s, r], r_r.at[s, r], (d, goal[r])).wait_recv()
        sums = nn(tmat[...], rrecv[s].reshape(NE * BLK, CH))
        mix = sums[0:T] + sums[T:2 * T]
        back = sums[2 * T:3 * T]
        if s < NS - 1:
            zsend[s, 0] = mix.astype(BF16)
            zsend[s, 1] = back.astype(BF16)
            for n in range(2):
                if s == 1:
                    for w in range(2):
                        slot = 3 + 2 * par + w
                        dev = (targets[s][n] * 4 + (h + w) % 2 * 2 + c, e)
                        part = zsend.at[s, n, :, windows[w]]
                        go(remote(part, yrecv.at[slot], k_s.at[n, w], y_r.at[slot], dev))
                    continue
                go(remote(zsend.at[s, n], zrecv.at[z], z_s.at[s, n], z_r.at[z], zdev(targets[s][n])))
        else:
            zsend[s, 0] = jnp.where(mine, back, mix).astype(BF16)
            for n, (src, dev) in enumerate((
                (zsend.at[s, 0, :, windows[0]], zdev(last_to)),
                (zsend.at[s, 0, :, windows[1]], last_to_over),
            )):
                go(remote(src, yrecv.at[n], y_s.at[n], y_r.at[n], dev))
            return jnp.where(mine, mix, back)

    give_back(1, 2)
    weight_grads(0)
    to_tokens(0)
    weight_grads(1)
    to_tokens(1)
    weight_grads(2)
    weight_grads(3)
    total = to_tokens(NS - 1)
    for k in range(1, NZ):
        zz = at_z(k)
        remote(gzrecv.at[zz], gzrecv.at[zz], gz_s.at[k], gz_r.at[zz], zdev(zz)).wait_recv()
    gc_sum = gzrecv[0]
    for k in range(1, NZ):
        gc_sum = gc_sum + gzrecv[k]
    gycs[0] = gc_sum
    gy = remote(gycs.at[0], gycs.at[1], p_s.at[0], p_r.at[0], over)
    gy.start()
    for k in (4, jnp.where(c == 0, up, down)):
        zz = at_z(NZ - k)
        remote(zsend.at[0, 0], zrecv.at[zz], z_s.at[0, 0], z_r.at[zz], zdev(zz)).wait_recv()
        total = total + zrecv[zz].astype(F32)
    ysend[...] = total.astype(BF16)
    yc = remote(ysend.at[:, windows[1]], yrecv.at[2], y_s.at[2], y_r.at[2], over)
    yc.start()
    gy.wait_recv()
    gc_sum = gc_sum + gycs[1]
    gycs[2] = gc_sum
    gx = remote(gycs.at[2], gycs.at[3], p_s.at[1], p_r.at[1], twin)
    gx.start()
    for n in range(7):
        remote(yrecv.at[n], yrecv.at[n], y_s.at[0], y_r.at[n], over).wait_recv()
    window = jnp.where(h == 0, total[:, 0:2 * T], total[:, T:3 * T])
    for n in range(7):
        window = window + yrecv[n].astype(F32)
    final = window.astype(BF16)
    fsend[...] = final
    fc = remote(fsend, frecv, p_s.at[2], p_r.at[2], twin)
    fc.start()
    shift = 64 * h + 96 * c
    pick = (iota((T, 2 * T), 1) == iota((T, 2 * T), 0) + shift).astype(F32).astype(BF16)
    gx.wait_recv()
    gc_sum = gc_sum + gycs[3]
    gcomb_ref[...] = gc_sum[0:2]
    a = nt(pick, final)
    fc.wait_recv()
    b = nt(pick, frecv[...])
    mixed_ref[...] = jnp.where(mine, a, b)[0:96].astype(BF16)
    gtok_ref[...] = jnp.where(mine, b, a)[0:96].astype(BF16)

    for cp in sends:
        cp.wait_send()
    for cp in (gy, yc, gx, fc):
        cp.wait_send()


def settle_kernel(*refs):
    copies = [pltpu.make_async_copy(refs[i], refs[6 + i], refs[12].at[i]) for i in range(6)]
    for cp in copies:
        cp.start()
    for cp in copies:
        cp.wait()


def settle(*arrays):
    any_spec = pl.BlockSpec(memory_space=pl.ANY)
    return pl.pallas_call(
        settle_kernel,
        out_shape=tuple(jax.ShapeDtypeStruct(a.shape, a.dtype) for a in arrays),
        in_specs=[any_spec] * 6,
        out_specs=(any_spec,) * 6,
        scratch_shapes=[pltpu.SemaphoreType.DMA((6,))],
        compiler_params=pltpu.CompilerParams(vmem_limit_bytes=16 * 1024 * 1024),
        name="settle",
    )(*arrays)


def local(tokens, expert_ids, combine, cotangent, w_gate, w_up, w_down):
    any_spec = pl.BlockSpec(memory_space=pl.ANY)
    vmem = pl.BlockSpec(memory_space=pltpu.VMEM)
    dma = pltpu.SemaphoreType.DMA
    mixed, gtok, gcomb, gg, gu, gd = pl.pallas_call(
        kernel,
        out_shape=(
            pltpu.VMEM((96, T), BF16),
            pltpu.VMEM((96, T), BF16),
            pltpu.VMEM((2, T), F32),
            pltpu.VMEM((D, W), BF16),
            pltpu.VMEM((D, W), BF16),
            pltpu.VMEM((W, D), BF16),
        ),
        in_specs=[any_spec, vmem, vmem, any_spec, any_spec, any_spec, any_spec],
        out_specs=(vmem,) * 6,
        scratch_shapes=[
            pltpu.VMEM((2 * T, QD), BF16),
            pltpu.VMEM((2 * T, QD), BF16),
            pltpu.VMEM((D, W), BF16),
            pltpu.VMEM((D, W), BF16),
            pltpu.VMEM((W, D), BF16),
            pltpu.VMEM((NP, CH, W), BF16),
            pltpu.VMEM((NP, CH, W), BF16),
            pltpu.VMEM((NP, W, CH), BF16),
            pltpu.VMEM((NE, 2 * T), F32),
            pltpu.VMEM((NE, 2 * T), F32),
            pltpu.VMEM((NE, BLK, QD), BF16),
            pltpu.VMEM((3, BLK, QD), BF16),
            pltpu.VMEM((2, 2, NE, BLK, QD), BF16),
            pltpu.VMEM((3, NE * CAP, W), BF16),
            pltpu.VMEM((3, NE * CAP, W), BF16),
            pltpu.VMEM((NE, CAP, T), F32),
            pltpu.VMEM((NE, CAP, T), F32),
            pltpu.VMEM((3 * T, NE * BLK), BF16),
            pltpu.VMEM((2, NE * CAP, CH), BF16),
            pltpu.VMEM((2, NE * CAP, CH), BF16),
            pltpu.VMEM((NS, NE, BLK, CH), BF16),
            pltpu.VMEM((NS, NE, BLK, CH), BF16),
            pltpu.VMEM((NS, 2, T, CH), BF16),
            pltpu.VMEM((NZ, T, CH), BF16),
            pltpu.VMEM((NZ, 8, T), F32),
            pltpu.VMEM((T, CH), BF16),
            pltpu.VMEM((7, T, 2 * T), BF16),
            pltpu.VMEM((4, 8, T), F32),
            pltpu.VMEM((T, 2 * T), BF16),
            pltpu.VMEM((T, 2 * T), BF16),
            dma((7,)),
            dma((3, NP)),
            dma((3, NP)),
            dma((NE,)),
            dma((NE,)),
            dma((NE,)),
            dma((NE,)),
            dma((2, 8)),
            dma((2, NE)),
            dma((2, 8)),
            dma((2, NE)),
            dma((2,)),
            dma((2,)),
            dma((NE,)),
            dma((NE,)),
            dma((2, 2)),
            dma((2, 2)),
            dma((NS, NE)),
            dma((NS, NE)),
            dma((NS, 2)),
            dma((NZ,)),
            dma((NZ,)),
            dma((NZ,)),
            dma((2, 2)),
            dma((3,)),
            dma((7,)),
            dma((3,)),
            dma((3,)),
        ],
        compiler_params=pltpu.CompilerParams(
            collective_id=0, has_side_effects=True, vmem_limit_bytes=59 * 1024 * 1024
        ),
        name="moe_layer",
    )(tokens, expert_ids.T, combine.T, cotangent, w_gate[0], w_up[0], w_down[0])
    mixed, gtok, gcomb, gg, gu, gd = settle(mixed, gtok, gcomb, gg, gu, gd)
    return mixed.T, gtok.T, gcomb.T, gg[None], gu[None], gd[None]


def solution(mesh):
    in_specs = (
        P("expert", None),
        P("expert", None),
        P("expert", None),
        P("expert", None),
        P("expert", None, "dp"),
        P("expert", None, "dp"),
        P("expert", "dp", None),
    )
    out_specs = (
        P("expert", "dp"),
        P("expert", "dp"),
        P("expert", None),
        P("expert", None, "dp"),
        P("expert", None, "dp"),
        P("expert", "dp", None),
    )
    return jax.shard_map(local, mesh=mesh, in_specs=in_specs, out_specs=out_specs, check_vma=False)
```
